32 devices in a mesh: dp: 4 (over x, core), tm: 8 (over z, y).
Axes of the slice: x: 2, y: 2, z: 4, core: 2. Of those that a mesh axis runs over, the one named last changes fastest.
Arguments:
- queries: bfloat16 [4, 2048, 1152], P('dp', 'tm'), may hold values from -96 to 96
- keys: bfloat16 [4, 2048, 1152], P('dp', 'tm'), may hold values from -6 to 6
- values: bfloat16 [4, 2048, 1152], P('dp', 'tm'), may hold values from -6 to 6
- out_grad: bfloat16 [4, 2048, 1152], P('dp', 'tm'), may hold values from -6 to 6
- lengths: int32 [4], P('dp'), may hold values from 512 to 2048, as said below
- rel_bias: float32 [12, 768], replicated, may hold values from -4 to 4
Outputs:
- query_grad: bfloat16 [4, 2048, 1152], P('dp', 'tm')
- key_grad: bfloat16 [4, 2048, 1152], P('dp', 'tm')
- value_grad: bfloat16 [4, 2048, 1152], P('dp', 'tm')
- bias_grad: float32 [12, 768], replicated
The draws below stay inside these ranges and needn't reach their ends.
Inputs may be any that keep to these rules, and one draw needn't show every extreme that they name: Every recording's valid frames are its first lengths[r] frames; some recording is valid to its end.
All inputs are finite; a program needn't handle non-finite values.
Results may differ from the reference program's by a relative error of at most 0.007.
Values may be sent and summed in bfloat16 or wider, within the bound.
No kernel may reach another device: no remote copies, remote signals or barrier semaphores. Data moves between devices by JAX's collectives and lax.ppermute only.
A program may use at most 128 MiB of HBM per device.

```python
import jax
import jax.numpy as jnp
from jax import lax

BLOCK = 256
HEADS = 12
HW = 1152
FRAMES = 2048
RECS = 4
OFFSETS = 768


def shared_keys(key):
    drawn = jax.random.normal(jax.random.fold_in(key, 101), (RECS, FRAMES, HW), jnp.float32)
    return jnp.clip(drawn, -6.0, 6.0)


def draw_keys(key, part):
    base_keys = shared_keys(key)
    return base_keys.astype(jnp.bfloat16)


def draw_queries(key, part):
    key = jax.random.fold_in(key, 2)
    fresh = jax.random.normal(key, (RECS, FRAMES, HW), jnp.float32)
    return jnp.clip(fresh, -96.0, 96.0).astype(jnp.bfloat16)


def draw_lengths(key, part):
    key = jax.random.fold_in(key, 3)
    drawn = jax.random.randint(key, (RECS,), FRAMES // 4, FRAMES + 1, dtype=jnp.int32)
    full_one = jax.random.randint(jax.random.fold_in(key, 1), (), 0, RECS, dtype=jnp.int32)
    return jnp.where(jnp.arange(RECS, dtype=jnp.int32) == full_one, FRAMES, drawn).astype(jnp.int32)


def shard_levels(stream_key, dims, split, low, high):
    def one(axis_at, shards_of):
        heights = jax.random.uniform(jax.random.fold_in(jax.random.fold_in(stream_key, 6), axis_at), (shards_of,), jnp.float32, low / len(split), high / len(split))
        return jnp.repeat(jnp.exp(heights), dims[axis_at] // shards_of).reshape((-1,) + (1,) * (len(dims) - axis_at - 1))

    level = one(*split[0])
    for cut in split[1:]:
        level = level * one(*cut)
    return level


def noise(rng, dims, width, bound, pieces=(), kind=jnp.bfloat16):
    factor_of = shard_levels(rng, dims, pieces, -0.22, 0.18) if pieces else 1.0
    entries = jax.random.normal(rng, dims, jnp.float32) * width * factor_of
    return jnp.minimum(jnp.maximum(entries, -bound), bound).astype(kind)


def setup_inputs(seed: int = 0) -> dict:
    seeds = jax.random.split(jax.random.key(seed), 7)
    queries = draw_queries(jax.random.fold_in(seeds[6], 71), 0)
    keys = draw_keys(jax.random.fold_in(seeds[6], 71), 0)
    values = noise(seeds[2], (RECS, FRAMES, HW), 1.0, 6.0, ((0, 4), (1, 8)))
    out_grad = noise(seeds[3], (RECS, FRAMES, HW), 1.0, 6.0, ((0, 4), (1, 8)))
    lengths = draw_lengths(jax.random.fold_in(seeds[6], 71), 0)
    rel_bias = noise(seeds[5], (HEADS, OFFSETS), 1.0, 4.0, (), jnp.float32)
    return dict(queries=queries, keys=keys, values=values, out_grad=out_grad, lengths=lengths, rel_bias=rel_bias)


masked_score = -1000000000.0

def toeplitz(vector, block_len):
    head_count = vector.shape[0]
    padded = jnp.pad(vector, ((0, 0), (0, 1)))
    repeated = jnp.broadcast_to(padded[:, None, :], (head_count, block_len, 2 * block_len))
    flattened = repeated.reshape(head_count, 2 * block_len * block_len)
    sliced = flattened[:, block_len - 1:block_len - 1 + block_len * (2 * block_len - 1)]
    return sliced.reshape(head_count, block_len, 2 * block_len - 1)[:, :, :block_len]

def diag_sums(matrix):
    head_count, block_len = (matrix.shape[0], matrix.shape[1])
    widened = jnp.pad(matrix, ((0, 0), (0, 0), (0, block_len - 1)))
    flattened = widened.reshape(head_count, block_len * (2 * block_len - 1))
    flattened = jnp.pad(flattened, ((0, 0), (block_len - 1, 1)))
    folded = flattened.reshape(head_count, block_len, 2 * block_len)
    return lax.optimization_barrier(jnp.sum(folded, axis=1))[:, :2 * block_len - 1]

def table_grad(left_sums, own_sums, block_len):
    return jnp.pad(left_sums, ((0, 0), (0, block_len + 1))) + jnp.pad(own_sums, ((0, 0), (block_len, 1)))

def rounded(array):
    return lax.optimization_barrier(array.astype(jnp.bfloat16)).astype(jnp.float32)

def reference(queries, keys, values, out_grad, lengths, rel_bias):
    record_count, frames, feature_width = queries.shape
    head_count = rel_bias.shape[0]
    head_width = feature_width // head_count
    block_len = BLOCK
    block_count = frames // block_len
    scaling = head_width ** (-0.5)
    bias_own = toeplitz(rel_bias[:, block_len:3 * block_len - 1], block_len)
    bias_left = toeplitz(rel_bias[:, :2 * block_len - 1], block_len)

    def one_record(packed):
        query_rec, key_rec, value_rec, grad_rec, length = packed
        frame_pos = jnp.arange(frames, dtype=jnp.int32)
        grad_rec = jnp.where((frame_pos < length)[:, None], grad_rec, jnp.zeros_like(grad_rec))
        shape = (block_count, block_len, head_count, head_width)
        query_blocks = query_rec.astype(jnp.float32).reshape(shape)
        key_blocks = key_rec.astype(jnp.float32).reshape(shape)
        value_blocks = value_rec.astype(jnp.float32).reshape(shape)
        grad_blocks = grad_rec.astype(jnp.float32).reshape(shape)
        zero_block = jnp.zeros((1, block_len, head_count, head_width), jnp.float32)
        key_prev = jnp.concatenate([zero_block, key_blocks[:-1]], axis=0)
        value_prev = jnp.concatenate([zero_block, value_blocks[:-1]], axis=0)
        block_ids = jnp.arange(block_count, dtype=jnp.int32)

        def one_block(items):
            query_here, key_here, key_before, value_here, value_before, grad_here, block_id = items
            own_frames = block_id * block_len + jnp.arange(block_len, dtype=jnp.int32)
            own_live = own_frames < length
            left_frames = own_frames - block_len
            left_live = (left_frames >= 0) & (left_frames < length)
            scores_own = jnp.einsum('qhe,khe->hqk', query_here, key_here) * scaling + bias_own
            scores_own = jnp.where(own_live[None, None, :], scores_own, masked_score)
            scores_left = jnp.einsum('qhe,khe->hqk', query_here, key_before) * scaling + bias_left
            scores_left = jnp.where(left_live[None, None, :], scores_left, masked_score)
            scores = jnp.concatenate([scores_left, scores_own], axis=2)
            row_top = lax.optimization_barrier(jnp.max(scores, axis=2, keepdims=True))
            expo = jnp.exp(scores - row_top)
            probs = expo / lax.optimization_barrier(jnp.sum(expo, axis=2, keepdims=True))
            value_window = jnp.concatenate([value_before, value_here], axis=0)
            dprobs = jnp.einsum('qhe,khe->hqk', grad_here, value_window)
            row_delta = lax.optimization_barrier(jnp.sum(probs * dprobs, axis=2, keepdims=True))
            dscores = probs * (dprobs - row_delta)
            probs_b = rounded(probs)
            dscores_b = rounded(dscores)
            query_grad = scaling * (jnp.einsum('hqk,khe->qhe', dscores_b[:, :, block_len:], key_here) + jnp.einsum('hqk,khe->qhe', dscores_b[:, :, :block_len], key_before))
            key_own = scaling * jnp.einsum('hqk,qhe->khe', dscores_b[:, :, block_len:], query_here)
            key_cross = rounded(scaling * jnp.einsum('hqk,qhe->khe', dscores_b[:, :, :block_len], query_here))
            value_own = jnp.einsum('hqk,qhe->khe', probs_b[:, :, block_len:], grad_here)
            value_cross = rounded(jnp.einsum('hqk,qhe->khe', probs_b[:, :, :block_len], grad_here))
            table = table_grad(diag_sums(dscores[:, :, :block_len]), diag_sums(dscores[:, :, block_len:]), block_len)
            return (query_grad, key_own, key_cross, value_own, value_cross, table)
        results = lax.map(one_block, (query_blocks, key_blocks, key_prev, value_blocks, value_prev, grad_blocks, block_ids))
        query_grad, key_own, key_cross, value_own, value_cross, tables = results
        key_next = jnp.concatenate([key_cross[1:], jnp.zeros_like(key_cross[:1])], axis=0)
        value_next = jnp.concatenate([value_cross[1:], jnp.zeros_like(value_cross[:1])], axis=0)
        query_out = query_grad.astype(jnp.bfloat16).reshape(frames, feature_width)
        key_out = (key_own + key_next).astype(jnp.bfloat16).reshape(frames, feature_width)
        value_out = (value_own + value_next).astype(jnp.bfloat16).reshape(frames, feature_width)
        return (query_out, key_out, value_out, lax.optimization_barrier(jnp.sum(tables, axis=0)))
    query_all, key_all, value_all, tables = lax.map(one_record, (queries, keys, values, out_grad, lengths))
    return (query_all, key_all, value_all, lax.optimization_barrier(jnp.sum(tables, axis=0)))
```

```python
import functools

import jax
import jax.numpy as jnp
import numpy as np
from jax import lax
from jax.experimental import pallas as pl
from jax.experimental.pallas import tpu as pltpu
from jax.sharding import PartitionSpec as P

BLOCK = 256
HALF = jnp.bfloat16
LOG2E = float(np.log2(np.e))
MASKED = -(2.0**30)
GROUP_HEADS = 4
GROUP_LANES = 384
WINDOWS = ((0, 128), (0, 256), (128, 256), (256, 128))

NT = (((1,), (1,)), ((), ()))
NN = (((1,), (0,)), ((), ()))
TN = (((0,), (0,)), ((), ()))


def dot(a, b, dims):
    return lax.dot_general(a, b, dims, preferred_element_type=jnp.float32)


def shifted(x, axis, by):
    count = lax.axis_size(axis)
    pairs = [(i, i + by) for i in range(count) if 0 <= i + by < count]
    return lax.ppermute(x, axis, pairs)


def head_mask(j, head_width, dtype):
    lo, width = WINDOWS[j]
    lane = lax.broadcasted_iota(jnp.int32, (1, width), 1) + lo
    inside = (lane >= j * head_width) & (lane < (j + 1) * head_width)
    return jnp.where(inside, 1.0, 0.0).astype(dtype)


def live_rows(count, width, dtype):
    row = lax.broadcasted_iota(jnp.int32, (BLOCK, width), 0)
    return jnp.where(row < count, 1.0, 0.0).astype(dtype)


def skew(row):
    base = pltpu.roll(jnp.broadcast_to(row, (8, 2 * BLOCK)), 0, 1, stride=1, stride_axis=0)
    turns = [pltpu.roll(base, 8 * a, 1) if a else base for a in range(16)]
    near = [turn[:, BLOCK:] for turn in turns]
    far = [turn[:, BLOCK - 128 : 2 * BLOCK - 128] for turn in turns]
    return jnp.concatenate(near + far, axis=0)


def unskew(matrix):
    zeros = jnp.zeros((8, 128), jnp.float32)
    total = None
    for a in range(16):
        upper = matrix[8 * a : 8 * a + 8]
        lower = matrix[128 + 8 * a : 136 + 8 * a]
        part = jnp.concatenate(
            [zeros, lower[:, :128], upper[:, :128] + lower[:, 128:], upper[:, 128:]], axis=1
        )
        if a:
            part = pltpu.roll(part, 2 * BLOCK - 8 * a, 1)
        total = part if total is None else total + part
    return total


def flipped(rows):
    tiles = rows.shape[1] // 128
    a = lax.broadcasted_iota(jnp.int32, (128, 128), 0)
    b = lax.broadcasted_iota(jnp.int32, (128, 128), 1)
    swap = jnp.where(a + b == 127, 1.0, 0.0).astype(jnp.bfloat16)
    total = None
    for _ in range(3):
        piece = rows.astype(jnp.bfloat16)
        rows = rows - piece.astype(jnp.float32)
        moved = jnp.concatenate(
            [dot(piece[:, 128 * t : 128 * t + 128], swap, NN) for t in reversed(range(tiles))], axis=1
        )
        total = moved if total is None else total + moved
    return total


def window(ref, j):
    lo, width = WINDOWS[j]
    return ref[:BLOCK, lo : lo + width]


def add_window(ref, j, value):
    lo, width = WINDOWS[j]
    for tile in range(0, width, 128):
        at = slice(lo + tile, lo + tile + 128)
        piece = value[:, tile : tile + 128]
        if (lo + tile) // 128 == j:
            ref[:, at] = piece
        else:
            ref[:, at] += piece


def live_tiles(count):
    rows = live_rows(count, 128, jnp.bfloat16)
    return {128: rows, 256: jnp.concatenate([rows, rows], axis=1)}


def put_lines(ref, j, lines):
    for tile in range(4):
        ref[0, tile, 8 * j : 8 * j + 8, :] = lines[:, 128 * tile : 128 * tile + 128]


def get_lines(ref, group, r):
    rows = pl.ds(r, GROUP_HEADS, stride=8)
    return jnp.concatenate([ref[group, tile, rows, :] for tile in range(4)], axis=1)


def lined(ref, group):
    total = get_lines(ref, group, 0)
    for r in range(1, 8):
        total = total + pltpu.roll(get_lines(ref, group, r), 2 * BLOCK - r, 1)
    return total


def pack_rows(ref, rows):
    high = rows.astype(HALF).astype(jnp.float32)
    low = rows - high
    main = jnp.concatenate([high[:12], low[4:8]], axis=0)
    side = jnp.concatenate([low[8:12, :128], low[8:12, 128:], jnp.zeros((8, 128), jnp.float32)], axis=0)
    ref[...] = jnp.concatenate([main, side], axis=1).astype(HALF)


def unpack_rows(ref):
    strip = ref[...].astype(jnp.float32)
    m = strip[:4, :BLOCK]
    total = strip[4:8, :BLOCK] + strip[12:16, :BLOCK]
    mixed = strip[8:12, :BLOCK] + jnp.concatenate([strip[:4, BLOCK:], strip[4:8, BLOCK:]], axis=1)
    return m, total, mixed


def reference_value(x):
    return jnp.max(x, axis=0, keepdims=True).astype(HALF).astype(jnp.float32)


def add_products(j, qm, gm, km, p, ds, dq_acc, dk_acc, dv_acc):
    pb = p.astype(HALF)
    dsb = ds.astype(HALF)
    add_window(dv_acc, j, dot(pb, gm, NN))
    add_window(dk_acc, j, dot(dsb, qm, NN))
    add_window(dq_acc, j, dot(dsb, km, TN))


def own_stats_kernel(
    head_width, group, live_ref, q_ref, g_ref, k_ref, v_ref, bias_ref, *refs
):
    if group == 0:
        stats_ref, e_ref, dp_ref, chunk_ref, flip_ref = refs
        flip_ref[...] = flipped(bias_ref[...]) * LOG2E
    else:
        stats_ref, e_ref, dp_ref, chunk_ref = refs[-4:]
        flip_ref = bias_ref

    scale = head_width**-0.5 * LOG2E
    live = live_ref[0]
    key_live = lax.broadcasted_iota(jnp.int32, (BLOCK, BLOCK), 0) < live
    rows = live_tiles(live)
    for j in range(GROUP_HEADS):
        mask = head_mask(j, head_width, HALF)
        head = group * GROUP_HEADS + j
        qm = window(q_ref, j) * mask
        gm = window(g_ref, j) * mask * rows[WINDOWS[j][1]]
        x = dot(window(k_ref, j), qm, NT) * scale + skew(flip_ref[head : head + 1, : 2 * BLOCK])
        x = jnp.where(key_live, x, MASKED)
        m = reference_value(x)
        e = jnp.exp2(x - m)
        dp = dot(window(v_ref, j), gm, NT)
        e_ref[j] = e
        dp_ref[j] = dp
        stats_ref[0, j : j + 1, :] = m
        stats_ref[0, 4 + j : 5 + j, :] = jnp.sum(e, axis=0, keepdims=True)
        stats_ref[0, 8 + j : 9 + j, :] = jnp.sum(e * dp, axis=0, keepdims=True)
    stats_ref[0, 12:16, :] = jnp.zeros((4, BLOCK), jnp.float32)
    chunk_ref[:BLOCK, :] = g_ref[...]
    pack_rows(chunk_ref.at[BLOCK:PACKED, :], stats_ref[0])


def cross_kernel(
    head_width, group, live_ref, q_ref, g_ref, k_ref, v_ref, w_ref, *refs
):
    out_ref, dq_ref, dk_ref, dv_ref, lines_ref, rows_ref, dq_acc, dk_acc, dv_acc = refs[-9:]
    scale = head_width**-0.5 * LOG2E
    live = live_tiles(live_ref[0])
    far_m, far_total, far_mixed = unpack_rows(g_ref.at[BLOCK:PACKED, :])
    for j in range(GROUP_HEADS):
        mask = head_mask(j, head_width, HALF)
        qm = window(q_ref, j) * mask
        gm = window(g_ref, j) * mask * live[WINDOWS[j][1]]
        km = window(k_ref, j) * mask
        x = dot(km, qm, NT) * scale + skew(w_ref[group * GROUP_HEADS + j : group * GROUP_HEADS + j + 1, BLOCK:])
        m_far = far_m[j : j + 1]
        m = jnp.maximum(reference_value(x), m_far)
        e = jnp.exp2(x - m)
        dp = dot(window(v_ref, j), gm, NT)
        shrink = jnp.exp2(m_far - m)
        total = jnp.sum(e, axis=0, keepdims=True) + far_total[j : j + 1] * shrink
        mixed = jnp.sum(e * dp, axis=0, keepdims=True) + far_mixed[j : j + 1] * shrink
        inverse = 1.0 / total
        delta = mixed * inverse
        rows_ref[j : j + 1, :] = m
        rows_ref[4 + j : 5 + j, :] = inverse
        rows_ref[8 + j : 9 + j, :] = delta
        p = e * inverse
        ds = p * (dp - delta)
        put_lines(lines_ref, j, unskew(ds))
        add_products(j, qm, gm, km, p, ds, dq_acc, dk_acc, dv_acc)
    rows_ref[12:16, :] = jnp.zeros((4, BLOCK), jnp.float32)
    pack_rows(out_ref, rows_ref[...])
    scaling = head_width**-0.5
    dq_ref[...] = (dq_acc[...] * scaling).astype(HALF)
    dk_ref[...] = (dk_acc[...] * scaling).astype(HALF)
    dv_ref[...] = dv_acc[...].astype(HALF)


ROW_TILES = 3 * BLOCK // 128


def place(row, tile, parts):
    each = parts[2] // 128
    at = row * ROW_TILES + tile
    return at // each, slice(128 * (at % each), 128 * (at % each) + 128)


def spread_kernel(terms_ref, out_ref):
    total = terms_ref[0]
    for part in range(1, terms_ref.shape[0]):
        total = total + terms_ref[part]
    for part in range(out_ref.shape[0]):
        out_ref[part] = total


def gather_kernel(parts_ref, _, out_ref):
    for row in range(out_ref.shape[0]):
        for tile in range(ROW_TILES):
            part, lanes = place(row, tile, parts_ref.shape)
            out_ref[row : row + 1, 128 * tile : 128 * tile + 128] = parts_ref[part, :, lanes]


def own_kernel(
    groups, head_width, live_ref, q_ref, g_ref, k_ref, e_ref, dp_ref, near_ref, given_ref, dkc_ref, dvc_ref,
    cross_ref, dq_ref, dk_ref, dv_ref, table_ref, dq_acc, dk_acc, dv_acc, lines_ref,
):
    step = pl.program_id(0)
    live = live_tiles(live_ref[0])
    given_m, given_inverse, given_delta = unpack_rows(given_ref)
    for j in range(GROUP_HEADS):
        mask = head_mask(j, head_width, HALF)
        qm = window(q_ref, j) * mask
        gm = window(g_ref, j) * mask * live[WINDOWS[j][1]]
        km = window(k_ref, j) * mask
        m_near = near_ref[0, j : j + 1, :]
        inverse_near = 1.0 / near_ref[0, 4 + j : 5 + j, :]
        inverse = given_inverse[j : j + 1]
        there = inverse > 0.0
        m = jnp.where(there, given_m[j : j + 1], m_near)
        ratio = jnp.exp2(m_near - m) * jnp.where(there, inverse, inverse_near)
        delta = jnp.where(there, given_delta[j : j + 1], near_ref[0, 8 + j : 9 + j, :] * inverse_near)
        p = e_ref[j] * ratio
        ds = p * (dp_ref[j] - delta)
        put_lines(lines_ref.at[pl.ds(step, 1)], j, unskew(ds))
        add_products(j, qm, gm, km, p, ds, dq_acc, dk_acc, dv_acc)
    scaling = head_width**-0.5
    f32 = jnp.float32
    dq_ref[...] = dq_acc[...] * scaling
    dk_ref[...] = (dk_acc[...] * scaling + dkc_ref[...].astype(f32)).astype(HALF)
    dv_ref[...] = (dv_acc[...] + dvc_ref[...].astype(f32)).astype(HALF)

    @pl.when(step == groups - 1)
    def _():
        table_ref[...] = jnp.zeros_like(table_ref)
        for i in range(groups):
            a, b = lined(lines_ref, i), lined(cross_ref, i)
            row = jnp.concatenate([a[:, :BLOCK], a[:, BLOCK:] + b[:, :BLOCK], b[:, BLOCK:]], axis=1)
            row = flipped(row)
            for j in range(GROUP_HEADS):
                for tile in range(ROW_TILES):
                    part, lanes = place(i * GROUP_HEADS + j, tile, table_ref.shape)
                    table_ref[part, :, lanes] = row[j : j + 1, 128 * tile : 128 * tile + 128]


def params(mebibytes=32):
    return pltpu.CompilerParams(vmem_limit_bytes=mebibytes * 1024 * 1024)


COST = pl.CostEstimate(flops=1024, bytes_accessed=1024, transcendentals=0)
LONG = pl.CostEstimate(flops=10**11, bytes_accessed=1024, transcendentals=0)


def shape(s, t=jnp.float32):
    return jax.ShapeDtypeStruct(s, t)


SMEM = pl.BlockSpec(memory_space=pltpu.SMEM)
ANY = pl.BlockSpec(memory_space=pl.ANY)
ACCS = [pltpu.VMEM((BLOCK, GROUP_LANES), jnp.float32)] * 3
PACKED = BLOCK + 16
LINES = (1, 4, 8 * GROUP_HEADS, 128)


def whole_spec(s):
    return pl.BlockSpec(s, lambda i: (0,) * len(s))


def columns(first=0):
    return pl.BlockSpec((BLOCK, GROUP_LANES), lambda i: (0, first + i))


def stack(size, *rest, first=0):
    return pl.BlockSpec((size,) + rest, lambda i: (first + i,) + (0,) * len(rest))


def columns(first=0, rows=BLOCK):
    return pl.BlockSpec((rows, GROUP_LANES), lambda i: (0, first + i))


def stack(size, *rest, first=0):
    return pl.BlockSpec((size,) + rest, lambda i: (first + i,) + (0,) * len(rest))


def own_stats(head_width, group, live, q, g, k, v, bias, before):
    heads = bias.shape[0]
    groups = heads // GROUP_HEADS
    squares = stack(GROUP_HEADS, BLOCK, BLOCK, first=group)
    outs = [
        shape((groups, 16, BLOCK)),
        shape((heads, BLOCK, BLOCK)),
        shape((heads, BLOCK, BLOCK)),
        shape((PACKED, GROUP_LANES), HALF),
    ]
    out_specs = [stack(1, 16, BLOCK, first=group), squares, squares, whole_spec((PACKED, GROUP_LANES))]
    if not before:
        outs.append(shape(bias.shape))
        out_specs.append(whole_spec(bias.shape))
    return pl.pallas_call(
        functools.partial(own_stats_kernel, head_width, group),
        grid=(1,),
        in_specs=[SMEM] + [columns(group)] * 4 + [whole_spec(bias.shape)] + [ANY] * len(before),
        out_specs=out_specs,
        out_shape=outs,
        input_output_aliases={6 + i: i for i in range(len(before))},
        compiler_params=params(60),
        cost_estimate=COST,
        name=f"own_stats_{group}",
    )(live, q, g, k, v, bias, *before)


def cross(head_width, group, live, q, g, k, v, w, before):
    half = shape(q.shape, HALF)
    groups = q.shape[1] // GROUP_LANES
    return pl.pallas_call(
        functools.partial(cross_kernel, head_width, group),
        grid=(1,),
        in_specs=[
            SMEM, columns(group), columns(rows=PACKED), columns(group), columns(group), whole_spec(w.shape),
        ] + [ANY] * len(before),
        out_specs=[columns(group, 16), columns(group), columns(group), columns(group), stack(*LINES, first=group)],
        out_shape=[shape((16, q.shape[1]), HALF), half, half, half, shape((groups,) + LINES[1:])],
        scratch_shapes=[pltpu.VMEM((16, BLOCK), jnp.float32)] + ACCS,
        input_output_aliases={6 + i: i for i in range(len(before))},
        compiler_params=params(),
        cost_estimate=COST,
        name=f"cross_{group}",
    )(live, q, g, k, v, w, *before)


def own(head_width, live, q, g, k, e, dp, near, given, dkc, dvc, lines, parts):
    groups = near.shape[0]
    table = shape((parts, 1, -(-groups * GROUP_HEADS * ROW_TILES // parts) * 128))
    return pl.pallas_call(
        functools.partial(own_kernel, groups, head_width),
        grid=(groups,),
        in_specs=[
            SMEM, columns(), columns(), columns(),
            stack(GROUP_HEADS, BLOCK, BLOCK), stack(GROUP_HEADS, BLOCK, BLOCK),
            stack(1, 16, BLOCK), columns(rows=16), columns(), columns(), whole_spec(lines.shape),
        ],
        out_specs=[columns()] * 3 + [whole_spec(table.shape)],
        out_shape=[shape(q.shape), shape(q.shape, HALF), shape(q.shape, HALF), table],
        scratch_shapes=ACCS + [pltpu.VMEM(lines.shape, jnp.float32)],
        compiler_params=params(),
        cost_estimate=LONG,
        name="own",
    )(live, q, g, k, e, dp, near, given, dkc, dvc, lines)


def spread(terms, count):
    return pl.pallas_call(
        spread_kernel,
        out_shape=shape((count,) + terms.shape[1:]),
        compiler_params=params(),
        cost_estimate=COST,
        name="spread",
    )(terms)


def sum_over_devices(parts, axes, heads, after):
    terms = lax.all_to_all(parts, axes, 0, 0)
    every = lax.all_to_all(spread(terms, parts.shape[0]), axes, 0, 0)
    return pl.pallas_call(
        gather_kernel,
        in_specs=[pl.BlockSpec(memory_space=pltpu.VMEM), ANY],
        out_shape=shape((heads, 3 * BLOCK)),
        compiler_params=params(),
        cost_estimate=COST,
        name="gather",
    )(every, after)


def per_device(queries, keys, values, out_grad, lengths, rel_bias):
    frame_count, feature_width = queries.shape[1:]
    head_count = rel_bias.shape[0]
    head_width = feature_width // head_count
    groups = head_count // GROUP_HEADS
    live_own = lengths - lax.axis_index("tm") * BLOCK
    live_next = live_own - BLOCK
    q, k, v, g = (a.reshape(frame_count, feature_width) for a in (queries, keys, values, out_grad))

    q_next = shifted(q, "tm", -1)
    *before, chunk, w = own_stats(head_width, 0, live_own, q, g, k, v, rel_bias, ())
    chunks = [shifted(chunk, "tm", -1)]
    for group in range(1, groups):
        *before, chunk = own_stats(head_width, group, live_own, q, g, k, v, w, before)
        chunks.append(shifted(chunk, "tm", -1))
    near, e, dp = before
    results = ()
    for group in range(groups):
        results = cross(head_width, group, live_next, q_next, chunks[group], k, v, w, results)
    given, dq_cross, dkc, dvc, lines = results
    given = shifted(given, "tm", 1)
    dq_cross = shifted(dq_cross, "tm", 1)
    parts = lax.axis_size("dp") * lax.axis_size("tm")
    dq_own, dk, dv, table = own(head_width, live_own, q, g, k, e, dp, near, given, dkc, dvc, lines, parts)
    dq = (dq_own + dq_cross.astype(jnp.float32)).astype(HALF)
    bias_grad = sum_over_devices(table, ("dp", "tm"), head_count, dq)
    return tuple(a[None] for a in (dq, dk, dv)) + (bias_grad,)


def solution(mesh):
    block = P("dp", "tm", None)
    return jax.shard_map(
        per_device,
        mesh=mesh,
        in_specs=(block, block, block, block, P("dp"), P()),
        out_specs=(block, block, block, P()),
        check_vma=False,
    )
```

```python
import functools

import jax
import jax.numpy as jnp
import numpy as np
from jax import lax
from jax.experimental import pallas as pl
from jax.experimental.pallas import tpu as pltpu
from jax.sharding import PartitionSpec as P

BLOCK = 256
HALF = jnp.bfloat16
LOG2E = float(np.log2(np.e))
MASKED = -(2.0**30)
GROUP_HEADS = 4
GROUP_LANES = 384
WIDTH = 256
FIRST = (0, 0, 128, 128)

NT = (((1,), (1,)), ((), ()))
NN = (((1,), (0,)), ((), ()))
TN = (((0,), (0,)), ((), ()))


def dot(a, b, dims):
    return lax.dot_general(a, b, dims, preferred_element_type=jnp.float32)


def shifted(x, axis, by):
    count = lax.axis_size(axis)
    pairs = [(i, i + by) for i in range(count) if 0 <= i + by < count]
    return lax.ppermute(x, axis, pairs)


def head_mask(j, head_width, dtype):
    lane = lax.broadcasted_iota(jnp.int32, (1, WIDTH), 1) + FIRST[j]
    inside = (lane >= j * head_width) & (lane < (j + 1) * head_width)
    return jnp.where(inside, 1.0, 0.0).astype(dtype)


def skew(row):
    base = pltpu.roll(jnp.broadcast_to(row, (8, 2 * BLOCK)), 0, 1, stride=1, stride_axis=0)
    turns = [pltpu.roll(base, 8 * a, 1) if a else base for a in range(16)]
    near = [turn[:, BLOCK:] for turn in turns]
    far = [turn[:, BLOCK - 128 : 2 * BLOCK - 128] for turn in turns]
    return jnp.concatenate(near + far, axis=0)


def unskew(matrix):
    zeros = jnp.zeros((8, 128), jnp.float32)
    total = None
    for a in range(16):
        upper = matrix[8 * a : 8 * a + 8]
        lower = matrix[128 + 8 * a : 136 + 8 * a]
        part = jnp.concatenate(
            [zeros, lower[:, :128], upper[:, :128] + lower[:, 128:], upper[:, 128:]], axis=1
        )
        if a:
            part = pltpu.roll(part, 2 * BLOCK - 8 * a, 1)
        total = part if total is None else total + part
    return total


def flipped(rows):
    tiles = rows.shape[1] // 128
    a = lax.broadcasted_iota(jnp.int32, (128, 128), 0)
    b = lax.broadcasted_iota(jnp.int32, (128, 128), 1)
    swap = jnp.where(a + b == 127, 1.0, 0.0).astype(jnp.bfloat16)
    total = None
    for _ in range(3):
        piece = rows.astype(jnp.bfloat16)
        rows = rows - piece.astype(jnp.float32)
        moved = jnp.concatenate(
            [dot(piece[:, 128 * t : 128 * t + 128], swap, NN) for t in reversed(range(tiles))], axis=1
        )
        total = moved if total is None else total + moved
    return total


def window(ref, j, group=0):
    first = group * GROUP_LANES + FIRST[j]
    return ref[:BLOCK, first : first + WIDTH]


def live_rows(count):
    row = lax.broadcasted_iota(jnp.int32, (BLOCK, WIDTH), 0)
    return jnp.where(row < count, 1.0, 0.0).astype(HALF)


def put_lines(ref, j, lines):
    for tile in range(4):
        ref[0, tile, 8 * j : 8 * j + 8, :] = lines[:, 128 * tile : 128 * tile + 128]


def get_lines(ref, group, r):
    rows = pl.ds(r, GROUP_HEADS, stride=8)
    return jnp.concatenate([ref[group, tile, rows, :] for tile in range(4)], axis=1)


def lined(ref, group):
    total = get_lines(ref, group, 0)
    for r in range(1, 8):
        total = total + pltpu.roll(get_lines(ref, group, r), 2 * BLOCK - r, 1)
    return total


def pack_rows(ref, rows):
    high = rows.astype(HALF).astype(jnp.float32)
    low = rows - high
    main = jnp.concatenate([high[:12], low[4:8]], axis=0)
    side = jnp.concatenate([low[8:12, :128], low[8:12, 128:], jnp.zeros((8, 128), jnp.float32)], axis=0)
    ref[...] = jnp.concatenate([main, side], axis=1).astype(HALF)


def unpack_rows(ref):
    strip = ref[...].astype(jnp.float32)
    m = strip[:4, :BLOCK]
    total = strip[4:8, :BLOCK] + strip[12:16, :BLOCK]
    mixed = strip[8:12, :BLOCK] + jnp.concatenate([strip[:4, BLOCK:], strip[4:8, BLOCK:]], axis=1)
    return m, total, mixed


def reference_value(x):
    return jnp.max(x, axis=0, keepdims=True).astype(HALF).astype(jnp.float32)


def pair_products(heads, dq_acc, dk_acc, dv_acc):
    for pair in range(2):
        qm, gm, km, p, ds = zip(*heads[2 * pair : 2 * pair + 2])
        ps, dss = (jnp.concatenate(x, axis=1) for x in (p, ds))
        products = (
            (dv_acc, dot(ps, jnp.concatenate(gm, axis=0), NN)),
            (dk_acc, dot(dss, jnp.concatenate(qm, axis=0), NN)),
            (dq_acc, dot(jnp.concatenate(ds, axis=0), jnp.concatenate(km, axis=0), TN)),
        )
        for ref, value in products:
            if pair == 0:
                ref[:, :WIDTH] = value
            else:
                ref[:, 128:WIDTH] += value[:, :128]
                ref[:, WIDTH:] = value[:, 128:]


def own_stats_kernel(
    head_width, group, live_ref, q_ref, g_ref, k_ref, v_ref, bias_ref, *refs
):
    if group == 0:
        stats_ref, e_ref, dp_ref, chunk_ref, flip_ref = refs
        flip_ref[...] = flipped(bias_ref[...]) * LOG2E
    else:
        stats_ref, e_ref, dp_ref, chunk_ref = refs[-4:]
        flip_ref = bias_ref

    scale = head_width**-0.5 * LOG2E
    live = live_ref[0]
    key_live = lax.broadcasted_iota(jnp.int32, (BLOCK, BLOCK), 0) < live
    rows = live_rows(live)
    for j in range(GROUP_HEADS):
        mask = head_mask(j, head_width, HALF)
        head = group * GROUP_HEADS + j
        qm = window(q_ref, j) * mask
        gm = window(g_ref, j) * mask * rows
        x = dot(window(k_ref, j), qm, NT) * scale + skew(flip_ref[head : head + 1, : 2 * BLOCK])
        x = jnp.where(key_live, x, MASKED)
        m = reference_value(x)
        e = jnp.exp2(x - m)
        dp = dot(window(v_ref, j), gm, NT)
        e_ref[j] = e
        dp_ref[j] = dp
        stats_ref[0, j : j + 1, :] = m
        stats_ref[0, 4 + j : 5 + j, :] = jnp.sum(e, axis=0, keepdims=True)
        stats_ref[0, 8 + j : 9 + j, :] = jnp.sum(e * dp, axis=0, keepdims=True)
    stats_ref[0, 12:16, :] = jnp.zeros((4, BLOCK), jnp.float32)
    chunk_ref[:BLOCK, :] = g_ref[...]
    pack_rows(chunk_ref.at[BLOCK:PACKED, :], stats_ref[0])


def cross_kernel(
    head_width, group, live_ref, q_ref, g_ref, k_ref, v_ref, w_ref, *refs
):
    out_ref, dq_ref, dk_ref, dv_ref, lines_ref, rows_ref, dq_acc, dk_acc, dv_acc = refs[-9:]
    scale = head_width**-0.5 * LOG2E
    live = live_rows(live_ref[0])
    far_m, far_total, far_mixed = unpack_rows(g_ref.at[BLOCK:PACKED, :])
    heads = []
    for j in range(GROUP_HEADS):
        mask = head_mask(j, head_width, HALF)
        qm = window(q_ref, j, group) * mask
        gm = window(g_ref, j) * mask * live
        km = window(k_ref, j, group) * mask
        x = dot(km, qm, NT) * scale + skew(w_ref[group * GROUP_HEADS + j : group * GROUP_HEADS + j + 1, BLOCK:])
        m_far = far_m[j : j + 1]
        m = jnp.maximum(reference_value(x), m_far)
        e = jnp.exp2(x - m)
        dp = dot(window(v_ref, j, group), gm, NT)
        shrink = jnp.exp2(m_far - m)
        total = jnp.sum(e, axis=0, keepdims=True) + far_total[j : j + 1] * shrink
        mixed = jnp.sum(e * dp, axis=0, keepdims=True) + far_mixed[j : j + 1] * shrink
        inverse = 1.0 / total
        delta = mixed * inverse
        rows_ref[j : j + 1, :] = m
        rows_ref[4 + j : 5 + j, :] = inverse
        rows_ref[8 + j : 9 + j, :] = delta
        p = e * inverse
        ds = p * (dp - delta)
        put_lines(lines_ref, j, unskew(ds))
        heads.append((qm, gm, km, p.astype(HALF), ds.astype(HALF)))
    pair_products(heads, dq_acc, dk_acc, dv_acc)
    rows_ref[12:16, :] = jnp.zeros((4, BLOCK), jnp.float32)
    pack_rows(out_ref, rows_ref[...])
    scaling = head_width**-0.5
    dq_ref[...] = (dq_acc[...] * scaling).astype(HALF)
    dk_ref[...] = (dk_acc[...] * scaling).astype(HALF)
    dv_ref[...] = dv_acc[...].astype(HALF)


ROW_TILES = 3 * BLOCK // 128


def place(row, tile, parts):
    each = parts[2] // 128
    at = row * ROW_TILES + tile
    return at // each, slice(128 * (at % each), 128 * (at % each) + 128)


def spread_kernel(terms_ref, out_ref):
    total = terms_ref[0]
    for part in range(1, terms_ref.shape[0]):
        total = total + terms_ref[part]
    for part in range(out_ref.shape[0]):
        out_ref[part] = total


def gather_kernel(parts_ref, _, out_ref):
    for row in range(out_ref.shape[0]):
        for tile in range(ROW_TILES):
            part, lanes = place(row, tile, parts_ref.shape)
            out_ref[row : row + 1, 128 * tile : 128 * tile + 128] = parts_ref[part, :, lanes]


def own_kernel(
    groups, head_width, live_ref, q_ref, g_ref, k_ref, e_ref, dp_ref, near_ref, given_ref, dkc_ref, dvc_ref,
    cross_ref, dq_ref, dk_ref, dv_ref, table_ref, dq_acc, dk_acc, dv_acc, lines_ref,
):
    step = pl.program_id(0)
    live = live_rows(live_ref[0])

    def one_group(group):
        lanes = slice(group * GROUP_LANES, (group + 1) * GROUP_LANES)
        given_m, given_inverse, given_delta = unpack_rows(given_ref.at[:, lanes])
        heads = []
        for j in range(GROUP_HEADS):
            mask = head_mask(j, head_width, HALF)
            head = group * GROUP_HEADS + j
            qm = window(q_ref, j, group) * mask
            gm = window(g_ref, j, group) * mask * live
            km = window(k_ref, j, group) * mask
            m_near = near_ref[group, j : j + 1, :]
            inverse_near = 1.0 / near_ref[group, 4 + j : 5 + j, :]
            inverse = given_inverse[j : j + 1]
            there = inverse > 0.0
            m = jnp.where(there, given_m[j : j + 1], m_near)
            ratio = jnp.exp2(m_near - m) * jnp.where(there, inverse, inverse_near)
            delta = jnp.where(there, given_delta[j : j + 1], near_ref[group, 8 + j : 9 + j, :] * inverse_near)
            p = e_ref[head] * ratio
            ds = p * (dp_ref[head] - delta)
            put_lines(lines_ref.at[group : group + 1], j, unskew(ds))
            heads.append((qm, gm, km, p.astype(HALF), ds.astype(HALF)))
        pair_products(heads, dq_acc, dk_acc, dv_acc)
        scaling = head_width**-0.5
        f32 = jnp.float32
        dq_ref[...] = dq_acc[...] * scaling
        dk_ref[...] = (dk_acc[...] * scaling + dkc_ref[:, lanes].astype(f32)).astype(HALF)
        dv_ref[...] = (dv_acc[...] + dvc_ref[:, lanes].astype(f32)).astype(HALF)

    for group in range(groups):
        pl.when(step == group)(functools.partial(one_group, group))

    @pl.when(step == groups - 1)
    def _():
        table_ref[...] = jnp.zeros_like(table_ref)
        for i in range(groups):
            a, b = lined(lines_ref, i), lined(cross_ref, i)
            row = jnp.concatenate([a[:, :BLOCK], a[:, BLOCK:] + b[:, :BLOCK], b[:, BLOCK:]], axis=1)
            row = flipped(row)
            for j in range(GROUP_HEADS):
                for tile in range(ROW_TILES):
                    part, lanes = place(i * GROUP_HEADS + j, tile, table_ref.shape)
                    table_ref[part, :, lanes] = row[j : j + 1, 128 * tile : 128 * tile + 128]


def params(mebibytes=32):
    return pltpu.CompilerParams(vmem_limit_bytes=mebibytes * 1024 * 1024)


COST = pl.CostEstimate(flops=1024, bytes_accessed=1024, transcendentals=0)
LONG = pl.CostEstimate(flops=10**11, bytes_accessed=1024, transcendentals=0)


def shape(s, t=jnp.float32):
    return jax.ShapeDtypeStruct(s, t)


SMEM = pl.BlockSpec(memory_space=pltpu.SMEM)
ANY = pl.BlockSpec(memory_space=pl.ANY)
VMEM = pl.BlockSpec(memory_space=pltpu.VMEM)
ACCS = [pltpu.VMEM((BLOCK, GROUP_LANES), jnp.float32)] * 3
PACKED = BLOCK + 16
LINES = (1, 4, 8 * GROUP_HEADS, 128)


def whole_spec(s):
    return pl.BlockSpec(s, lambda i: (0,) * len(s))


def columns(first=0):
    return pl.BlockSpec((BLOCK, GROUP_LANES), lambda i: (0, first + i))


def stack(size, *rest, first=0):
    return pl.BlockSpec((size,) + rest, lambda i: (first + i,) + (0,) * len(rest))


def columns(first=0, rows=BLOCK):
    return pl.BlockSpec((rows, GROUP_LANES), lambda i: (0, first + i))


def stack(size, *rest, first=0):
    return pl.BlockSpec((size,) + rest, lambda i: (first + i,) + (0,) * len(rest))


def own_stats(head_width, group, live, q, g, k, v, bias, before):
    heads = bias.shape[0]
    groups = heads // GROUP_HEADS
    squares = stack(GROUP_HEADS, BLOCK, BLOCK, first=group)
    outs = [
        shape((groups, 16, BLOCK)),
        shape((heads, BLOCK, BLOCK)),
        shape((heads, BLOCK, BLOCK)),
        shape((PACKED, GROUP_LANES), HALF),
    ]
    out_specs = [stack(1, 16, BLOCK, first=group), squares, squares, whole_spec((PACKED, GROUP_LANES))]
    if not before:
        outs.append(shape(bias.shape))
        out_specs.append(whole_spec(bias.shape))
    return pl.pallas_call(
        functools.partial(own_stats_kernel, head_width, group),
        grid=(1,),
        in_specs=[SMEM] + [columns(group)] * 4 + [whole_spec(bias.shape)] + [ANY] * len(before),
        out_specs=out_specs,
        out_shape=outs,
        input_output_aliases={6 + i: i for i in range(len(before))},
        compiler_params=params(60),
        cost_estimate=COST,
        name=f"own_stats_{group}",
    )(live, q, g, k, v, bias, *before)


def cross(head_width, group, live, q, g, k, v, w, before):
    half = shape(q.shape, HALF)
    groups = q.shape[1] // GROUP_LANES
    return pl.pallas_call(
        functools.partial(cross_kernel, head_width, group),
        grid=(1,),
        in_specs=[SMEM] + [VMEM] * 5 + [ANY] * len(before),
        out_specs=[columns(group, 16), columns(group), columns(group), columns(group), stack(*LINES, first=group)],
        out_shape=[shape((16, q.shape[1]), HALF), half, half, half, shape((groups,) + LINES[1:])],
        scratch_shapes=[pltpu.VMEM((16, BLOCK), jnp.float32)] + ACCS,
        input_output_aliases={6 + i: i for i in range(len(before))},
        compiler_params=params(),
        cost_estimate=COST,
        name=f"cross_{group}",
    )(live, q, g, k, v, w, *before)


def own(head_width, live, q, g, k, e, dp, near, given, dkc, dvc, lines, parts):
    groups = near.shape[0]
    table = shape((parts, 1, -(-groups * GROUP_HEADS * ROW_TILES // parts) * 128))
    return pl.pallas_call(
        functools.partial(own_kernel, groups, head_width),
        grid=(groups,),
        in_specs=[SMEM] + [VMEM] * 10,
        out_specs=[columns()] * 3 + [whole_spec(table.shape)],
        out_shape=[shape(q.shape), shape(q.shape, HALF), shape(q.shape, HALF), table],
        scratch_shapes=ACCS + [pltpu.VMEM(lines.shape, jnp.float32)],
        compiler_params=params(),
        cost_estimate=LONG,
        name="own",
    )(live, q, g, k, e, dp, near, given, dkc, dvc, lines)


def spread(terms, count):
    return pl.pallas_call(
        spread_kernel,
        out_shape=shape((count,) + terms.shape[1:]),
        compiler_params=params(),
        cost_estimate=COST,
        name="spread",
    )(terms)


def sum_over_devices(parts, axes, heads, after):
    terms = lax.all_to_all(parts, axes, 0, 0)
    every = lax.all_to_all(spread(terms, parts.shape[0]), axes, 0, 0)
    return pl.pallas_call(
        gather_kernel,
        in_specs=[VMEM, ANY],
        out_shape=shape((heads, 3 * BLOCK)),
        compiler_params=params(),
        cost_estimate=COST,
        name="gather",
    )(every, after)


def per_device(queries, keys, values, out_grad, lengths, rel_bias):
    frame_count, feature_width = queries.shape[1:]
    head_count = rel_bias.shape[0]
    head_width = feature_width // head_count
    groups = head_count // GROUP_HEADS
    live_own = lengths - lax.axis_index("tm") * BLOCK
    live_next = live_own - BLOCK
    q, k, v, g = (a.reshape(frame_count, feature_width) for a in (queries, keys, values, out_grad))

    q_next = shifted(q, "tm", -1)
    *before, chunk, w = own_stats(head_width, 0, live_own, q, g, k, v, rel_bias, ())
    chunks = [shifted(chunk, "tm", -1)]
    for group in range(1, groups):
        *before, chunk = own_stats(head_width, group, live_own, q, g, k, v, w, before)
        chunks.append(shifted(chunk, "tm", -1))
    near, e, dp = before
    results = ()
    for group in range(groups):
        results = cross(head_width, group, live_next, q_next, chunks[group], k, v, w, results)
    given, dq_cross, dkc, dvc, lines = results
    given = shifted(given, "tm", 1)
    dq_cross = shifted(dq_cross, "tm", 1)
    parts = lax.axis_size("dp") * lax.axis_size("tm")
    dq_own, dk, dv, table = own(head_width, live_own, q, g, k, e, dp, near, given, dkc, dvc, lines, parts)
    dq = (dq_own + dq_cross.astype(jnp.float32)).astype(HALF)
    bias_grad = sum_over_devices(table, ("dp", "tm"), head_count, dq)
    return tuple(a[None] for a in (dq, dk, dv)) + (bias_grad,)


def solution(mesh):
    block = P("dp", "tm", None)
    return jax.shard_map(
        per_device,
        mesh=mesh,
        in_specs=(block, block, block, block, P("dp"), P()),
        out_specs=(block, block, block, P()),
        check_vma=False,
    )
```

```python
import functools

import jax
import jax.numpy as jnp
import numpy as np
from jax import lax
from jax.experimental import pallas as pl
from jax.experimental.pallas import tpu as pltpu
from jax.sharding import PartitionSpec as P

BLOCK = 256
HALF = jnp.bfloat16
LOG2E = float(np.log2(np.e))
MASKED = -(2.0**30)
GROUP_HEADS = 4
GROUP_LANES = 384
WIDTH = 256
FIRST = (0, 0, 128, 128)

NT = (((1,), (1,)), ((), ()))
NN = (((1,), (0,)), ((), ()))
TN = (((0,), (0,)), ((), ()))


def dot(a, b, dims):
    return lax.dot_general(a, b, dims, preferred_element_type=jnp.float32)


def shifted(x, axis, by):
    count = lax.axis_size(axis)
    pairs = [(i, i + by) for i in range(count) if 0 <= i + by < count]
    return lax.ppermute(x, axis, pairs)


def head_mask(j, head_width, dtype):
    lane = lax.broadcasted_iota(jnp.int32, (1, WIDTH), 1) + FIRST[j]
    inside = (lane >= j * head_width) & (lane < (j + 1) * head_width)
    return jnp.where(inside, 1.0, 0.0).astype(dtype)


def skew(row):
    base = pltpu.roll(jnp.broadcast_to(row, (8, 2 * BLOCK)), 0, 1, stride=1, stride_axis=0)
    turns = [pltpu.roll(base, 8 * a, 1) if a else base for a in range(16)]
    near = [turn[:, BLOCK:] for turn in turns]
    far = [turn[:, BLOCK - 128 : 2 * BLOCK - 128] for turn in turns]
    return jnp.concatenate(near + far, axis=0)


def unskew(matrix):
    zeros = jnp.zeros((8, 128), jnp.float32)
    total = None
    for a in range(16):
        upper = matrix[8 * a : 8 * a + 8]
        lower = matrix[128 + 8 * a : 136 + 8 * a]
        part = jnp.concatenate(
            [zeros, lower[:, :128], upper[:, :128] + lower[:, 128:], upper[:, 128:]], axis=1
        )
        if a:
            part = pltpu.roll(part, 2 * BLOCK - 8 * a, 1)
        total = part if total is None else total + part
    return total


def flipped(rows):
    tiles = rows.shape[1] // 128
    a = lax.broadcasted_iota(jnp.int32, (128, 128), 0)
    b = lax.broadcasted_iota(jnp.int32, (128, 128), 1)
    swap = jnp.where(a + b == 127, 1.0, 0.0).astype(jnp.bfloat16)
    total = None
    for _ in range(3):
        piece = rows.astype(jnp.bfloat16)
        rows = rows - piece.astype(jnp.float32)
        moved = jnp.concatenate(
            [dot(piece[:, 128 * t : 128 * t + 128], swap, NN) for t in reversed(range(tiles))], axis=1
        )
        total = moved if total is None else total + moved
    return total


def window(ref, j, group=0):
    first = group * GROUP_LANES + FIRST[j]
    return ref[:BLOCK, first : first + WIDTH]


def live_rows(count):
    row = lax.broadcasted_iota(jnp.int32, (BLOCK, WIDTH), 0)
    return jnp.where(row < count, 1.0, 0.0).astype(HALF)


def put_lines(ref, j, lines):
    for tile in range(4):
        ref[0, tile, 8 * j : 8 * j + 8, :] = lines[:, 128 * tile : 128 * tile + 128]


def get_lines(ref, group, r):
    rows = pl.ds(r, GROUP_HEADS, stride=8)
    return jnp.concatenate([ref[group, tile, rows, :] for tile in range(4)], axis=1)


def lined(ref, group):
    total = get_lines(ref, group, 0)
    for r in range(1, 8):
        total = total + pltpu.roll(get_lines(ref, group, r), 2 * BLOCK - r, 1)
    return total


def pack_rows(ref, rows):
    high = rows.astype(HALF).astype(jnp.float32)
    low = rows - high
    main = jnp.concatenate([high[:12], low[4:8]], axis=0)
    side = jnp.concatenate([low[8:12, :128], low[8:12, 128:], jnp.zeros((8, 128), jnp.float32)], axis=0)
    ref[...] = jnp.concatenate([main, side], axis=1).astype(HALF)


def unpack_rows(ref):
    strip = ref[...].astype(jnp.float32)
    m = strip[:4, :BLOCK]
    total = strip[4:8, :BLOCK] + strip[12:16, :BLOCK]
    mixed = strip[8:12, :BLOCK] + jnp.concatenate([strip[:4, BLOCK:], strip[4:8, BLOCK:]], axis=1)
    return m, total, mixed


def reference_value(x):
    return jnp.max(x, axis=0, keepdims=True).astype(HALF).astype(jnp.float32)


def pair_products(heads, dq_acc, dk_acc, dv_acc):
    for pair in range(2):
        qm, gm, km, p, ds = zip(*heads[2 * pair : 2 * pair + 2])
        ps, dss = (jnp.concatenate(x, axis=1) for x in (p, ds))
        products = (
            (dv_acc, dot(ps, jnp.concatenate(gm, axis=0), NN)),
            (dk_acc, dot(dss, jnp.concatenate(qm, axis=0), NN)),
            (dq_acc, dot(jnp.concatenate(ds, axis=0), jnp.concatenate(km, axis=0), TN)),
        )
        for ref, value in products:
            if pair == 0:
                ref[:, :WIDTH] = value
            else:
                ref[:, 128:WIDTH] += value[:, :128]
                ref[:, WIDTH:] = value[:, 128:]


def own_stats_kernel(
    head_width, group, live_ref, q_ref, g_ref, k_ref, v_ref, bias_ref, *refs
):
    if group == 0:
        stats_ref, e_ref, dp_ref, chunk_ref, flip_ref = refs
        flip_ref[...] = flipped(bias_ref[...]) * LOG2E
    else:
        stats_ref, e_ref, dp_ref, chunk_ref = refs[-4:]
        flip_ref = bias_ref

    scale = head_width**-0.5 * LOG2E
    live = live_ref[0]
    key_live = lax.broadcasted_iota(jnp.int32, (BLOCK, BLOCK), 0) < live
    rows = live_rows(live)
    for j in range(GROUP_HEADS):
        mask = head_mask(j, head_width, HALF)
        head = group * GROUP_HEADS + j
        qm = window(q_ref, j) * mask
        gm = window(g_ref, j) * mask * rows
        x = dot(window(k_ref, j), qm, NT) * scale + skew(flip_ref[head : head + 1, : 2 * BLOCK])
        x = jnp.where(key_live, x, MASKED)
        m = reference_value(x)
        e = jnp.exp2(x - m)
        dp = dot(window(v_ref, j), gm, NT)
        e_ref[j] = e
        dp_ref[j] = dp
        stats_ref[0, j : j + 1, :] = m
        stats_ref[0, 4 + j : 5 + j, :] = jnp.sum(e, axis=0, keepdims=True)
        stats_ref[0, 8 + j : 9 + j, :] = jnp.sum(e * dp, axis=0, keepdims=True)
    stats_ref[0, 12:16, :] = jnp.zeros((4, BLOCK), jnp.float32)
    chunk_ref[:BLOCK, :] = g_ref[...]
    pack_rows(chunk_ref.at[BLOCK:PACKED, :], stats_ref[0])


def cross_kernel(
    head_width, group, live_ref, q_ref, g_ref, k_ref, v_ref, w_ref, *refs
):
    out_ref, dq_ref, dk_ref, dv_ref, lines_ref, rows_ref, dq_acc, dk_acc, dv_acc = refs[-9:]
    scale = head_width**-0.5 * LOG2E
    live = live_rows(live_ref[0])
    far_m, far_total, far_mixed = unpack_rows(g_ref.at[BLOCK:PACKED, :])
    heads = []
    for j in range(GROUP_HEADS):
        mask = head_mask(j, head_width, HALF)
        qm = window(q_ref, j, group) * mask
        gm = window(g_ref, j) * mask * live
        km = window(k_ref, j, group) * mask
        x = dot(km, qm, NT) * scale + skew(w_ref[group * GROUP_HEADS + j : group * GROUP_HEADS + j + 1, BLOCK:])
        m_far = far_m[j : j + 1]
        m = jnp.maximum(reference_value(x), m_far)
        e = jnp.exp2(x - m)
        dp = dot(window(v_ref, j, group), gm, NT)
        shrink = jnp.exp2(m_far - m)
        total = jnp.sum(e, axis=0, keepdims=True) + far_total[j : j + 1] * shrink
        mixed = jnp.sum(e * dp, axis=0, keepdims=True) + far_mixed[j : j + 1] * shrink
        inverse = 1.0 / total
        delta = mixed * inverse
        rows_ref[j : j + 1, :] = m
        rows_ref[4 + j : 5 + j, :] = inverse
        rows_ref[8 + j : 9 + j, :] = delta
        p = e * inverse
        ds = p * (dp - delta)
        put_lines(lines_ref, j, unskew(ds))
        heads.append((qm, gm, km, p.astype(HALF), ds.astype(HALF)))
    pair_products(heads, dq_acc, dk_acc, dv_acc)
    rows_ref[12:16, :] = jnp.zeros((4, BLOCK), jnp.float32)
    pack_rows(out_ref, rows_ref[...])
    scaling = head_width**-0.5
    dq_ref[...] = (dq_acc[...] * scaling).astype(HALF)
    dk_ref[...] = (dk_acc[...] * scaling).astype(HALF)
    dv_ref[...] = dv_acc[...].astype(HALF)


ROW_TILES = 3 * BLOCK // 128


def place(row, tile, parts):
    each = parts[2] // 128
    at = row * ROW_TILES + tile
    return at // each, slice(128 * (at % each), 128 * (at % each) + 128)


def spread_kernel(terms_ref, out_ref):
    total = terms_ref[0]
    for part in range(1, terms_ref.shape[0]):
        total = total + terms_ref[part]
    for part in range(out_ref.shape[0]):
        out_ref[part] = total


def gather_kernel(count, every_ref, _, out_ref):
    terms = every_ref.shape[0] // count
    shape_of_parts = (count,) + every_ref.shape[1:]
    totals = []
    for part in range(count):
        total = every_ref[part * terms]
        for term in range(1, terms):
            total = total + every_ref[part * terms + term]
        totals.append(total)
    for row in range(out_ref.shape[0]):
        for tile in range(ROW_TILES):
            part, lanes = place(row, tile, shape_of_parts)
            out_ref[row : row + 1, 128 * tile : 128 * tile + 128] = totals[part][:, lanes]


def own_kernel(
    groups, head_width, live_ref, q_ref, g_ref, k_ref, e_ref, dp_ref, near_ref, given_ref, dkc_ref, dvc_ref,
    cross_ref, dq_ref, dk_ref, dv_ref, table_ref, dq_acc, dk_acc, dv_acc, lines_ref,
):
    step = pl.program_id(0)
    live = live_rows(live_ref[0])

    def one_group(group):
        lanes = slice(group * GROUP_LANES, (group + 1) * GROUP_LANES)
        given_m, given_inverse, given_delta = unpack_rows(given_ref.at[:, lanes])
        heads = []
        for j in range(GROUP_HEADS):
            mask = head_mask(j, head_width, HALF)
            head = group * GROUP_HEADS + j
            qm = window(q_ref, j, group) * mask
            gm = window(g_ref, j, group) * mask * live
            km = window(k_ref, j, group) * mask
            m_near = near_ref[group, j : j + 1, :]
            inverse_near = 1.0 / near_ref[group, 4 + j : 5 + j, :]
            inverse = given_inverse[j : j + 1]
            there = inverse > 0.0
            m = jnp.where(there, given_m[j : j + 1], m_near)
            ratio = jnp.exp2(m_near - m) * jnp.where(there, inverse, inverse_near)
            delta = jnp.where(there, given_delta[j : j + 1], near_ref[group, 8 + j : 9 + j, :] * inverse_near)
            p = e_ref[head] * ratio
            ds = p * (dp_ref[head] - delta)
            put_lines(lines_ref.at[group : group + 1], j, unskew(ds))
            heads.append((qm, gm, km, p.astype(HALF), ds.astype(HALF)))
        pair_products(heads, dq_acc, dk_acc, dv_acc)
        scaling = head_width**-0.5
        f32 = jnp.float32
        dq_ref[...] = dq_acc[...] * scaling
        dk_ref[...] = (dk_acc[...] * scaling + dkc_ref[:, lanes].astype(f32)).astype(HALF)
        dv_ref[...] = (dv_acc[...] + dvc_ref[:, lanes].astype(f32)).astype(HALF)

    for group in range(groups):
        pl.when(step == group)(functools.partial(one_group, group))

    @pl.when(step == groups - 1)
    def _():
        table_ref[...] = jnp.zeros_like(table_ref)
        for i in range(groups):
            a, b = lined(lines_ref, i), lined(cross_ref, i)
            row = jnp.concatenate([a[:, :BLOCK], a[:, BLOCK:] + b[:, :BLOCK], b[:, BLOCK:]], axis=1)
            row = flipped(row)
            for j in range(GROUP_HEADS):
                for tile in range(ROW_TILES):
                    part, lanes = place(i * GROUP_HEADS + j, tile, table_ref.shape)
                    table_ref[part, :, lanes] = row[j : j + 1, 128 * tile : 128 * tile + 128]


def params(mebibytes=32):
    return pltpu.CompilerParams(vmem_limit_bytes=mebibytes * 1024 * 1024)


COST = pl.CostEstimate(flops=1024, bytes_accessed=1024, transcendentals=0)
LONG = pl.CostEstimate(flops=10**11, bytes_accessed=1024, transcendentals=0)


def shape(s, t=jnp.float32):
    return jax.ShapeDtypeStruct(s, t)


SMEM = pl.BlockSpec(memory_space=pltpu.SMEM)
ANY = pl.BlockSpec(memory_space=pl.ANY)
VMEM = pl.BlockSpec(memory_space=pltpu.VMEM)
ACCS = [pltpu.VMEM((BLOCK, GROUP_LANES), jnp.float32)] * 3
PACKED = BLOCK + 16
LINES = (1, 4, 8 * GROUP_HEADS, 128)


def whole_spec(s):
    return pl.BlockSpec(s, lambda i: (0,) * len(s))


def columns(first=0):
    return pl.BlockSpec((BLOCK, GROUP_LANES), lambda i: (0, first + i))


def stack(size, *rest, first=0):
    return pl.BlockSpec((size,) + rest, lambda i: (first + i,) + (0,) * len(rest))


def columns(first=0, rows=BLOCK):
    return pl.BlockSpec((rows, GROUP_LANES), lambda i: (0, first + i))


def stack(size, *rest, first=0):
    return pl.BlockSpec((size,) + rest, lambda i: (first + i,) + (0,) * len(rest))


def own_stats(head_width, group, live, q, g, k, v, bias, before):
    heads = bias.shape[0]
    groups = heads // GROUP_HEADS
    squares = stack(GROUP_HEADS, BLOCK, BLOCK, first=group)
    outs = [
        shape((groups, 16, BLOCK)),
        shape((heads, BLOCK, BLOCK)),
        shape((heads, BLOCK, BLOCK)),
        shape((PACKED, GROUP_LANES), HALF),
    ]
    out_specs = [stack(1, 16, BLOCK, first=group), squares, squares, whole_spec((PACKED, GROUP_LANES))]
    if not before:
        outs.append(shape(bias.shape))
        out_specs.append(whole_spec(bias.shape))
    return pl.pallas_call(
        functools.partial(own_stats_kernel, head_width, group),
        grid=(1,),
        in_specs=[SMEM] + [columns(group)] * 4 + [whole_spec(bias.shape)] + [ANY] * len(before),
        out_specs=out_specs,
        out_shape=outs,
        input_output_aliases={6 + i: i for i in range(len(before))},
        compiler_params=params(60),
        cost_estimate=COST,
        name=f"own_stats_{group}",
    )(live, q, g, k, v, bias, *before)


def cross(head_width, group, live, q, g, k, v, w, before):
    half = shape(q.shape, HALF)
    groups = q.shape[1] // GROUP_LANES
    return pl.pallas_call(
        functools.partial(cross_kernel, head_width, group),
        grid=(1,),
        in_specs=[SMEM] + [VMEM] * 5 + [ANY] * len(before),
        out_specs=[columns(group, 16), columns(group), columns(group), columns(group), stack(*LINES, first=group)],
        out_shape=[shape((16, q.shape[1]), HALF), half, half, half, shape((groups,) + LINES[1:])],
        scratch_shapes=[pltpu.VMEM((16, BLOCK), jnp.float32)] + ACCS,
        input_output_aliases={6 + i: i for i in range(len(before))},
        compiler_params=params(),
        cost_estimate=COST,
        name=f"cross_{group}",
    )(live, q, g, k, v, w, *before)


def own(head_width, live, q, g, k, e, dp, near, given, dkc, dvc, lines, parts):
    groups = near.shape[0]
    table = shape((parts, 1, -(-groups * GROUP_HEADS * ROW_TILES // parts) * 128))
    return pl.pallas_call(
        functools.partial(own_kernel, groups, head_width),
        grid=(groups,),
        in_specs=[SMEM] + [VMEM] * 10,
        out_specs=[columns()] * 3 + [whole_spec(table.shape)],
        out_shape=[shape(q.shape), shape(q.shape, HALF), shape(q.shape, HALF), table],
        scratch_shapes=ACCS + [pltpu.VMEM(lines.shape, jnp.float32)],
        compiler_params=params(),
        cost_estimate=LONG,
        name="own",
    )(live, q, g, k, e, dp, near, given, dkc, dvc, lines)


def spread(terms, count):
    return pl.pallas_call(
        spread_kernel,
        out_shape=shape((count,) + terms.shape[1:]),
        compiler_params=params(),
        cost_estimate=COST,
        name="spread",
    )(terms)


def sum_over_devices(parts, inner, outer, heads, after):
    count = parts.shape[0]
    terms = lax.all_to_all(parts, inner, 0, 0)
    sums = spread(terms, count * lax.axis_size(outer))
    every = lax.all_to_all(sums, (inner, outer), 0, 0)
    return pl.pallas_call(
        functools.partial(gather_kernel, count),
        in_specs=[VMEM, ANY],
        out_shape=shape((heads, 3 * BLOCK)),
        compiler_params=params(),
        cost_estimate=COST,
        name="gather",
    )(every, after)


def per_device(queries, keys, values, out_grad, lengths, rel_bias):
    frame_count, feature_width = queries.shape[1:]
    head_count = rel_bias.shape[0]
    head_width = feature_width // head_count
    groups = head_count // GROUP_HEADS
    live_own = lengths - lax.axis_index("tm") * BLOCK
    live_next = live_own - BLOCK
    q, k, v, g = (a.reshape(frame_count, feature_width) for a in (queries, keys, values, out_grad))

    q_next = shifted(q, "tm", -1)
    *before, chunk, w = own_stats(head_width, 0, live_own, q, g, k, v, rel_bias, ())
    chunks = [shifted(chunk, "tm", -1)]
    for group in range(1, groups):
        *before, chunk = own_stats(head_width, group, live_own, q, g, k, v, w, before)
        chunks.append(shifted(chunk, "tm", -1))
    near, e, dp = before
    results = ()
    for group in range(groups):
        results = cross(head_width, group, live_next, q_next, chunks[group], k, v, w, results)
    given, dq_cross, dkc, dvc, lines = results
    given = shifted(given, "tm", 1)
    dq_cross = shifted(dq_cross, "tm", 1)
    parts = lax.axis_size("dp")
    dq_own, dk, dv, table = own(head_width, live_own, q, g, k, e, dp, near, given, dkc, dvc, lines, parts)
    dq = (dq_own + dq_cross.astype(jnp.float32)).astype(HALF)
    bias_grad = sum_over_devices(table, "dp", "tm", head_count, dq)
    return tuple(a[None] for a in (dq, dk, dv)) + (bias_grad,)


def solution(mesh):
    block = P("dp", "tm", None)
    return jax.shard_map(
        per_device,
        mesh=mesh,
        in_specs=(block, block, block, block, P("dp"), P()),
        out_specs=(block, block, block, P()),
        check_vma=False,
    )
```

```python
import functools

import jax
import jax.numpy as jnp
import numpy as np
from jax import lax
from jax.experimental import pallas as pl
from jax.experimental.pallas import tpu as pltpu
from jax.sharding import PartitionSpec as P

BLOCK = 256
HALF = jnp.bfloat16
LOG2E = float(np.log2(np.e))
MASKED = -(2.0**30)
GROUP_HEADS = 4
GROUP_LANES = 384
WIDTH = 256
FIRST = (0, 0, 128, 128)

NT = (((1,), (1,)), ((), ()))
NN = (((1,), (0,)), ((), ()))
TN = (((0,), (0,)), ((), ()))


def dot(a, b, dims):
    return lax.dot_general(a, b, dims, preferred_element_type=jnp.float32)


def shifted(x, axis, by):
    count = lax.axis_size(axis)
    pairs = [(i, i + by) for i in range(count) if 0 <= i + by < count]
    return lax.ppermute(x, axis, pairs)


def head_mask(j, head_width, dtype):
    lane = lax.broadcasted_iota(jnp.int32, (1, WIDTH), 1) + FIRST[j]
    inside = (lane >= j * head_width) & (lane < (j + 1) * head_width)
    return jnp.where(inside, 1.0, 0.0).astype(dtype)


def skew(row):
    base = pltpu.roll(jnp.broadcast_to(row, (8, 2 * BLOCK)), 0, 1, stride=1, stride_axis=0)
    turns = [pltpu.roll(base, 8 * a, 1) if a else base for a in range(16)]
    near = [turn[:, BLOCK:] for turn in turns]
    far = [turn[:, BLOCK - 128 : 2 * BLOCK - 128] for turn in turns]
    return jnp.concatenate(near + far, axis=0)


def unskew(matrix):
    zeros = jnp.zeros((8, 128), jnp.float32)
    total = None
    for a in range(16):
        upper = matrix[8 * a : 8 * a + 8]
        lower = matrix[128 + 8 * a : 136 + 8 * a]
        part = jnp.concatenate(
            [zeros, lower[:, :128], upper[:, :128] + lower[:, 128:], upper[:, 128:]], axis=1
        )
        if a:
            part = pltpu.roll(part, 2 * BLOCK - 8 * a, 1)
        total = part if total is None else total + part
    return total


def flipped(rows):
    tiles = rows.shape[1] // 128
    a = lax.broadcasted_iota(jnp.int32, (128, 128), 0)
    b = lax.broadcasted_iota(jnp.int32, (128, 128), 1)
    swap = jnp.where(a + b == 127, 1.0, 0.0).astype(jnp.bfloat16)
    total = None
    for _ in range(3):
        piece = rows.astype(jnp.bfloat16)
        rows = rows - piece.astype(jnp.float32)
        moved = jnp.concatenate(
            [dot(piece[:, 128 * t : 128 * t + 128], swap, NN) for t in reversed(range(tiles))], axis=1
        )
        total = moved if total is None else total + moved
    return total


def window(ref, j, group=0):
    first = group * GROUP_LANES + FIRST[j]
    return ref[:BLOCK, first : first + WIDTH]


def live_rows(count):
    row = lax.broadcasted_iota(jnp.int32, (BLOCK, WIDTH), 0)
    return jnp.where(row < count, 1.0, 0.0).astype(HALF)


def put_lines(ref, j, lines):
    for tile in range(4):
        ref[0, tile, 8 * j : 8 * j + 8, :] = lines[:, 128 * tile : 128 * tile + 128]


def get_lines(ref, group, r):
    rows = pl.ds(r, GROUP_HEADS, stride=8)
    return jnp.concatenate([ref[group, tile, rows, :] for tile in range(4)], axis=1)


def lined(ref, group):
    total = get_lines(ref, group, 0)
    for r in range(1, 8):
        total = total + pltpu.roll(get_lines(ref, group, r), 2 * BLOCK - r, 1)
    return total


def pack_rows(ref, rows):
    high = rows.astype(HALF).astype(jnp.float32)
    low = rows - high
    main = jnp.concatenate([high[:12], low[4:8]], axis=0)
    side = jnp.concatenate([low[8:12, :128], low[8:12, 128:], jnp.zeros((8, 128), jnp.float32)], axis=0)
    ref[...] = jnp.concatenate([main, side], axis=1).astype(HALF)


def unpack_rows(ref):
    strip = ref[...].astype(jnp.float32)
    m = strip[:4, :BLOCK]
    total = strip[4:8, :BLOCK] + strip[12:16, :BLOCK]
    mixed = strip[8:12, :BLOCK] + jnp.concatenate([strip[:4, BLOCK:], strip[4:8, BLOCK:]], axis=1)
    return m, total, mixed


def reference_value(x):
    return jnp.max(x, axis=0, keepdims=True).astype(HALF).astype(jnp.float32)


def pair_products(heads, dq_acc, dk_acc, dv_acc):
    for pair in range(2):
        qm, gm, km, p, ds = zip(*heads[2 * pair : 2 * pair + 2])
        ps, dss = (jnp.concatenate(x, axis=1) for x in (p, ds))
        products = (
            (dv_acc, dot(ps, jnp.concatenate(gm, axis=0), NN)),
            (dk_acc, dot(dss, jnp.concatenate(qm, axis=0), NN)),
            (dq_acc, dot(jnp.concatenate(ds, axis=0), jnp.concatenate(km, axis=0), TN)),
        )
        for ref, value in products:
            if pair == 0:
                ref[:, :WIDTH] = value
            else:
                ref[:, 128:WIDTH] += value[:, :128]
                ref[:, WIDTH:] = value[:, 128:]


def own_stats_kernel(
    head_width, group, live_ref, q_ref, g_ref, k_ref, v_ref, bias_ref, *refs
):
    if group == 0:
        stats_ref, e_ref, dp_ref, chunk_ref, flip_ref = refs
        flip_ref[...] = flipped(bias_ref[...]) * LOG2E
    else:
        stats_ref, e_ref, dp_ref, chunk_ref = refs[-4:]
        flip_ref = bias_ref

    scale = head_width**-0.5 * LOG2E
    live = live_ref[0]
    key_live = lax.broadcasted_iota(jnp.int32, (BLOCK, BLOCK), 0) < live
    rows = live_rows(live)
    for j in range(GROUP_HEADS):
        mask = head_mask(j, head_width, HALF)
        head = group * GROUP_HEADS + j
        qm = window(q_ref, j) * mask
        gm = window(g_ref, j) * mask * rows
        x = dot(window(k_ref, j), qm, NT) * scale + skew(flip_ref[head : head + 1, : 2 * BLOCK])
        x = jnp.where(key_live, x, MASKED)
        m = reference_value(x)
        e = jnp.exp2(x - m)
        dp = dot(window(v_ref, j), gm, NT)
        e_ref[j] = e
        dp_ref[j] = dp
        stats_ref[0, j : j + 1, :] = m
        stats_ref[0, 4 + j : 5 + j, :] = jnp.sum(e, axis=0, keepdims=True)
        stats_ref[0, 8 + j : 9 + j, :] = jnp.sum(e * dp, axis=0, keepdims=True)
    stats_ref[0, 12:16, :] = jnp.zeros((4, BLOCK), jnp.float32)
    chunk_ref[:BLOCK, :] = g_ref[...]
    pack_rows(chunk_ref.at[BLOCK:PACKED, :], stats_ref[0])


def cross_kernel(
    head_width, group, live_ref, q_ref, g_ref, k_ref, v_ref, w_ref, *refs
):
    out_ref, dq_ref, dk_ref, dv_ref, lines_ref, rows_ref, dq_acc, dk_acc, dv_acc = refs[-9:]
    scale = head_width**-0.5 * LOG2E
    live = live_rows(live_ref[0])
    far_m, far_total, far_mixed = unpack_rows(g_ref.at[BLOCK:PACKED, :])
    heads = []
    for j in range(GROUP_HEADS):
        mask = head_mask(j, head_width, HALF)
        qm = window(q_ref, j, group) * mask
        gm = window(g_ref, j) * mask * live
        km = window(k_ref, j, group) * mask
        x = dot(km, qm, NT) * scale + skew(w_ref[group * GROUP_HEADS + j : group * GROUP_HEADS + j + 1, BLOCK:])
        m_far = far_m[j : j + 1]
        m = jnp.maximum(reference_value(x), m_far)
        e = jnp.exp2(x - m)
        dp = dot(window(v_ref, j, group), gm, NT)
        shrink = jnp.exp2(m_far - m)
        total = jnp.sum(e, axis=0, keepdims=True) + far_total[j : j + 1] * shrink
        mixed = jnp.sum(e * dp, axis=0, keepdims=True) + far_mixed[j : j + 1] * shrink
        inverse = 1.0 / total
        delta = mixed * inverse
        rows_ref[j : j + 1, :] = m
        rows_ref[4 + j : 5 + j, :] = inverse
        rows_ref[8 + j : 9 + j, :] = delta
        p = e * inverse
        ds = p * (dp - delta)
        put_lines(lines_ref, j, unskew(ds))
        heads.append((qm, gm, km, p.astype(HALF), ds.astype(HALF)))
    pair_products(heads, dq_acc, dk_acc, dv_acc)
    rows_ref[12:16, :] = jnp.zeros((4, BLOCK), jnp.float32)
    pack_rows(out_ref, rows_ref[...])
    scaling = head_width**-0.5
    dq_ref[...] = (dq_acc[...] * scaling).astype(HALF)
    dk_ref[...] = (dk_acc[...] * scaling).astype(HALF)
    dv_ref[...] = dv_acc[...].astype(HALF)


ROW_TILES = 3 * BLOCK // 128


def place(row, tile, parts):
    each = parts[2] // 128
    at = row * ROW_TILES + tile
    return at // each, slice(128 * (at % each), 128 * (at % each) + 128)


def spread_kernel(terms_ref, out_ref):
    total = terms_ref[0]
    for part in range(1, terms_ref.shape[0]):
        total = total + terms_ref[part]
    for part in range(out_ref.shape[0]):
        out_ref[part] = total


def gather_kernel(count, every_ref, _, out_ref):
    terms = every_ref.shape[0] // count
    shape_of_parts = (count,) + every_ref.shape[1:]
    totals = []
    for part in range(count):
        total = every_ref[part * terms]
        for term in range(1, terms):
            total = total + every_ref[part * terms + term]
        totals.append(total)
    for row in range(out_ref.shape[0]):
        for tile in range(ROW_TILES):
            part, lanes = place(row, tile, shape_of_parts)
            out_ref[row : row + 1, 128 * tile : 128 * tile + 128] = totals[part][:, lanes]


def own_parts(head, group, j, e_ref, dp_ref, near_ref, given):
    given_m, given_inverse, given_delta = given
    m_near = near_ref[group, j : j + 1, :]
    inverse_near = 1.0 / near_ref[group, 4 + j : 5 + j, :]
    inverse = given_inverse[j : j + 1]
    there = inverse > 0.0
    m = jnp.where(there, given_m[j : j + 1], m_near)
    ratio = jnp.exp2(m_near - m) * jnp.where(there, inverse, inverse_near)
    delta = jnp.where(there, given_delta[j : j + 1], near_ref[group, 8 + j : 9 + j, :] * inverse_near)
    p = e_ref[head] * ratio
    return p, p * (dp_ref[head] - delta)


def lanes_of(group):
    return slice(group * GROUP_LANES, (group + 1) * GROUP_LANES)


def table_kernel(groups, e_ref, dp_ref, near_ref, given_ref, cross_ref, table_ref, lines_ref):
    table_ref[...] = jnp.zeros_like(table_ref)
    for group in range(groups):
        given = unpack_rows(given_ref.at[:, lanes_of(group)])
        for j in range(GROUP_HEADS):
            _, ds = own_parts(group * GROUP_HEADS + j, group, j, e_ref, dp_ref, near_ref, given)
            put_lines(lines_ref.at[group : group + 1], j, unskew(ds))
        a, b = lined(lines_ref, group), lined(cross_ref, group)
        row = jnp.concatenate([a[:, :BLOCK], a[:, BLOCK:] + b[:, :BLOCK], b[:, BLOCK:]], axis=1)
        row = flipped(row)
        for j in range(GROUP_HEADS):
            for tile in range(ROW_TILES):
                part, lanes = place(group * GROUP_HEADS + j, tile, table_ref.shape)
                table_ref[part, :, lanes] = row[j : j + 1, 128 * tile : 128 * tile + 128]


def own_kernel(
    groups, head_width, live_ref, q_ref, g_ref, k_ref, e_ref, dp_ref, near_ref, given_ref, dqc_ref, dkc_ref, dvc_ref,
    dq_ref, dk_ref, dv_ref, dq_acc, dk_acc, dv_acc,
):
    live = live_rows(live_ref[0])

    def one_group(group):
        lanes = lanes_of(group)
        given = unpack_rows(given_ref.at[:, lanes])
        heads = []
        for j in range(GROUP_HEADS):
            mask = head_mask(j, head_width, HALF)
            qm = window(q_ref, j, group) * mask
            gm = window(g_ref, j, group) * mask * live
            km = window(k_ref, j, group) * mask
            p, ds = own_parts(group * GROUP_HEADS + j, group, j, e_ref, dp_ref, near_ref, given)
            heads.append((qm, gm, km, p.astype(HALF), ds.astype(HALF)))
        pair_products(heads, dq_acc, dk_acc, dv_acc)
        scaling = head_width**-0.5
        f32 = jnp.float32
        dq_ref[...] = (dq_acc[...] * scaling + dqc_ref[:, lanes].astype(f32)).astype(HALF)
        dk_ref[...] = (dk_acc[...] * scaling + dkc_ref[:, lanes].astype(f32)).astype(HALF)
        dv_ref[...] = (dv_acc[...] + dvc_ref[:, lanes].astype(f32)).astype(HALF)

    for group in range(groups):
        pl.when(pl.program_id(0) == group)(functools.partial(one_group, group))


def params(mebibytes=32):
    return pltpu.CompilerParams(vmem_limit_bytes=mebibytes * 1024 * 1024)


COST = pl.CostEstimate(flops=1024, bytes_accessed=1024, transcendentals=0)
LONG = pl.CostEstimate(flops=10**11, bytes_accessed=1024, transcendentals=0)


def shape(s, t=jnp.float32):
    return jax.ShapeDtypeStruct(s, t)


SMEM = pl.BlockSpec(memory_space=pltpu.SMEM)
ANY = pl.BlockSpec(memory_space=pl.ANY)
VMEM = pl.BlockSpec(memory_space=pltpu.VMEM)
ACCS = [pltpu.VMEM((BLOCK, GROUP_LANES), jnp.float32)] * 3
PACKED = BLOCK + 16
LINES = (1, 4, 8 * GROUP_HEADS, 128)


def whole_spec(s):
    return pl.BlockSpec(s, lambda i: (0,) * len(s))


def columns(first=0):
    return pl.BlockSpec((BLOCK, GROUP_LANES), lambda i: (0, first + i))


def stack(size, *rest, first=0):
    return pl.BlockSpec((size,) + rest, lambda i: (first + i,) + (0,) * len(rest))


def columns(first=0, rows=BLOCK):
    return pl.BlockSpec((rows, GROUP_LANES), lambda i: (0, first + i))


def stack(size, *rest, first=0):
    return pl.BlockSpec((size,) + rest, lambda i: (first + i,) + (0,) * len(rest))


def own_stats(head_width, group, live, q, g, k, v, bias, before):
    heads = bias.shape[0]
    groups = heads // GROUP_HEADS
    squares = stack(GROUP_HEADS, BLOCK, BLOCK, first=group)
    outs = [
        shape((groups, 16, BLOCK)),
        shape((heads, BLOCK, BLOCK)),
        shape((heads, BLOCK, BLOCK)),
        shape((PACKED, GROUP_LANES), HALF),
    ]
    out_specs = [stack(1, 16, BLOCK, first=group), squares, squares, whole_spec((PACKED, GROUP_LANES))]
    if not before:
        outs.append(shape(bias.shape))
        out_specs.append(whole_spec(bias.shape))
    return pl.pallas_call(
        functools.partial(own_stats_kernel, head_width, group),
        grid=(1,),
        in_specs=[SMEM] + [columns(group)] * 4 + [whole_spec(bias.shape)] + [ANY] * len(before),
        out_specs=out_specs,
        out_shape=outs,
        input_output_aliases={6 + i: i for i in range(len(before))},
        compiler_params=params(60),
        cost_estimate=COST,
        name=f"own_stats_{group}",
    )(live, q, g, k, v, bias, *before)


def cross(head_width, group, live, q, g, k, v, w, before):
    half = shape(q.shape, HALF)
    groups = q.shape[1] // GROUP_LANES
    return pl.pallas_call(
        functools.partial(cross_kernel, head_width, group),
        grid=(1,),
        in_specs=[SMEM] + [VMEM] * 5 + [ANY] * len(before),
        out_specs=[columns(group, 16), columns(group), columns(group), columns(group), stack(*LINES, first=group)],
        out_shape=[shape((16, q.shape[1]), HALF), half, half, half, shape((groups,) + LINES[1:])],
        scratch_shapes=[pltpu.VMEM((16, BLOCK), jnp.float32)] + ACCS,
        input_output_aliases={6 + i: i for i in range(len(before))},
        compiler_params=params(),
        cost_estimate=COST,
        name=f"cross_{group}",
    )(live, q, g, k, v, w, *before)


def table_sums(e, dp, near, given, lines, parts):
    groups = near.shape[0]
    return pl.pallas_call(
        functools.partial(table_kernel, groups),
        in_specs=[VMEM] * 5,
        out_shape=shape((parts, 1, -(-groups * GROUP_HEADS * ROW_TILES // parts) * 128)),
        scratch_shapes=[pltpu.VMEM(lines.shape, jnp.float32)],
        compiler_params=params(),
        cost_estimate=LONG,
        name="table_sums",
    )(e, dp, near, given, lines)


def own(head_width, live, q, g, k, e, dp, near, given, dqc, dkc, dvc):
    groups = near.shape[0]
    return pl.pallas_call(
        functools.partial(own_kernel, groups, head_width),
        grid=(groups,),
        in_specs=[SMEM] + [VMEM] * 10,
        out_specs=[columns()] * 3,
        out_shape=[shape(q.shape, HALF)] * 3,
        scratch_shapes=ACCS,
        compiler_params=params(),
        cost_estimate=LONG,
        name="own",
    )(live, q, g, k, e, dp, near, given, dqc, dkc, dvc)


def spread(terms, count):
    return pl.pallas_call(
        spread_kernel,
        out_shape=shape((count,) + terms.shape[1:]),
        compiler_params=params(),
        cost_estimate=COST,
        name="spread",
    )(terms)


def sum_over_devices(parts, inner, outer, heads, after):
    count = parts.shape[0]
    terms = lax.all_to_all(parts, inner, 0, 0)
    sums = spread(terms, count * lax.axis_size(outer))
    every = lax.all_to_all(sums, (inner, outer), 0, 0)
    return pl.pallas_call(
        functools.partial(gather_kernel, count),
        in_specs=[VMEM, ANY],
        out_shape=shape((heads, 3 * BLOCK)),
        compiler_params=params(),
        cost_estimate=COST,
        name="gather",
    )(every, after)


def per_device(queries, keys, values, out_grad, lengths, rel_bias):
    frame_count, feature_width = queries.shape[1:]
    head_count = rel_bias.shape[0]
    head_width = feature_width // head_count
    groups = head_count // GROUP_HEADS
    live_own = lengths - lax.axis_index("tm") * BLOCK
    live_next = live_own - BLOCK
    q, k, v, g = (a.reshape(frame_count, feature_width) for a in (queries, keys, values, out_grad))

    q_next = shifted(q, "tm", -1)
    *before, chunk, w = own_stats(head_width, 0, live_own, q, g, k, v, rel_bias, ())
    chunks = [shifted(chunk, "tm", -1)]
    for group in range(1, groups):
        *before, chunk = own_stats(head_width, group, live_own, q, g, k, v, w, before)
        chunks.append(shifted(chunk, "tm", -1))
    near, e, dp = before
    results = ()
    for group in range(groups):
        results = cross(head_width, group, live_next, q_next, chunks[group], k, v, w, results)
    given, dq_cross, dkc, dvc, lines = results
    given = shifted(given, "tm", 1)
    dq_cross = shifted(dq_cross, "tm", 1)
    parts = lax.axis_size("dp")
    table = table_sums(e, dp, near, given, lines, parts)
    dq, dk, dv = own(head_width, live_own, q, g, k, e, dp, near, given, dq_cross, dkc, dvc)
    bias_grad = sum_over_devices(table, "dp", "tm", head_count, dq)
    return tuple(a[None] for a in (dq, dk, dv)) + (bias_grad,)


def solution(mesh):
    block = P("dp", "tm", None)
    return jax.shard_map(
        per_device,
        mesh=mesh,
        in_specs=(block, block, block, block, P("dp"), P()),
        out_specs=(block, block, block, P()),
        check_vma=False,
    )
```

```python
import functools

import jax
import jax.numpy as jnp
import numpy as np
from jax import lax
from jax.experimental import pallas as pl
from jax.experimental.pallas import tpu as pltpu
from jax.sharding import PartitionSpec as P

BLOCK = 256
HALF = jnp.bfloat16
LOG2E = float(np.log2(np.e))
MASKED = -(2.0**30)
GROUP_HEADS = 4
GROUP_LANES = 384
WIDTH = 256
FIRST = (0, 0, 128, 128)

NT = (((1,), (1,)), ((), ()))
NN = (((1,), (0,)), ((), ()))
TN = (((0,), (0,)), ((), ()))


def dot(a, b, dims):
    return lax.dot_general(a, b, dims, preferred_element_type=jnp.float32)


def shifted(x, axis, by):
    count = lax.axis_size(axis)
    pairs = [(i, i + by) for i in range(count) if 0 <= i + by < count]
    return lax.ppermute(x, axis, pairs)


def head_mask(j, head_width, dtype):
    lane = lax.broadcasted_iota(jnp.int32, (1, WIDTH), 1) + FIRST[j]
    inside = (lane >= j * head_width) & (lane < (j + 1) * head_width)
    return jnp.where(inside, 1.0, 0.0).astype(dtype)


def skew(row):
    base = pltpu.roll(jnp.broadcast_to(row, (8, 2 * BLOCK)), 0, 1, stride=1, stride_axis=0)
    turns = [pltpu.roll(base, 8 * a, 1) if a else base for a in range(16)]
    near = [turn[:, BLOCK:] for turn in turns]
    far = [turn[:, BLOCK - 128 : 2 * BLOCK - 128] for turn in turns]
    return jnp.concatenate(near + far, axis=0)


def unskew(matrix):
    zeros = jnp.zeros((8, 128), jnp.float32)
    total = None
    for a in range(16):
        upper = matrix[8 * a : 8 * a + 8]
        lower = matrix[128 + 8 * a : 136 + 8 * a]
        part = jnp.concatenate(
            [zeros, lower[:, :128], upper[:, :128] + lower[:, 128:], upper[:, 128:]], axis=1
        )
        if a:
            part = pltpu.roll(part, 2 * BLOCK - 8 * a, 1)
        total = part if total is None else total + part
    return total


def flipped(rows):
    tiles = rows.shape[1] // 128
    a = lax.broadcasted_iota(jnp.int32, (128, 128), 0)
    b = lax.broadcasted_iota(jnp.int32, (128, 128), 1)
    swap = jnp.where(a + b == 127, 1.0, 0.0).astype(jnp.bfloat16)
    total = None
    for _ in range(3):
        piece = rows.astype(jnp.bfloat16)
        rows = rows - piece.astype(jnp.float32)
        moved = jnp.concatenate(
            [dot(piece[:, 128 * t : 128 * t + 128], swap, NN) for t in reversed(range(tiles))], axis=1
        )
        total = moved if total is None else total + moved
    return total


def window(ref, j, group=0):
    first = group * GROUP_LANES + FIRST[j]
    return ref[:BLOCK, first : first + WIDTH]


def live_rows(count):
    row = lax.broadcasted_iota(jnp.int32, (BLOCK, WIDTH), 0)
    return jnp.where(row < count, 1.0, 0.0).astype(HALF)


def put_lines(ref, j, lines):
    for tile in range(4):
        ref[0, tile, 8 * j : 8 * j + 8, :] = lines[:, 128 * tile : 128 * tile + 128]


def get_lines(ref, group, r):
    rows = pl.ds(r, GROUP_HEADS, stride=8)
    return jnp.concatenate([ref[group, tile, rows, :] for tile in range(4)], axis=1)


def lined(ref, group):
    total = get_lines(ref, group, 0)
    for r in range(1, 8):
        total = total + pltpu.roll(get_lines(ref, group, r), 2 * BLOCK - r, 1)
    return total


def pack_rows(ref, rows):
    high = rows.astype(HALF).astype(jnp.float32)
    low = rows - high
    main = jnp.concatenate([high[:12], low[4:8]], axis=0)
    side = jnp.concatenate([low[8:12, :128], low[8:12, 128:], jnp.zeros((8, 128), jnp.float32)], axis=0)
    ref[...] = jnp.concatenate([main, side], axis=1).astype(HALF)


def unpack_rows(ref):
    strip = ref[...].astype(jnp.float32)
    m = strip[:4, :BLOCK]
    total = strip[4:8, :BLOCK] + strip[12:16, :BLOCK]
    mixed = strip[8:12, :BLOCK] + jnp.concatenate([strip[:4, BLOCK:], strip[4:8, BLOCK:]], axis=1)
    return m, total, mixed


def reference_value(x):
    return jnp.max(x, axis=0, keepdims=True).astype(HALF).astype(jnp.float32)


def pair_products(heads, dq_acc, dk_acc, dv_acc):
    for pair in range(2):
        qm, gm, km, p, ds = zip(*heads[2 * pair : 2 * pair + 2])
        ps, dss = (jnp.concatenate(x, axis=1) for x in (p, ds))
        products = (
            (dv_acc, dot(ps, jnp.concatenate(gm, axis=0), NN)),
            (dk_acc, dot(dss, jnp.concatenate(qm, axis=0), NN)),
            (dq_acc, dot(jnp.concatenate(ds, axis=0), jnp.concatenate(km, axis=0), TN)),
        )
        for ref, value in products:
            if pair == 0:
                ref[:, :WIDTH] = value
            else:
                ref[:, 128:WIDTH] += value[:, :128]
                ref[:, WIDTH:] = value[:, 128:]


def own_stats_kernel(
    head_width, group, live_ref, q_ref, g_ref, k_ref, v_ref, bias_ref, *refs
):
    if group == 0:
        stats_ref, e_ref, dp_ref, chunk_ref, flip_ref = refs
        flip_ref[...] = flipped(bias_ref[...]) * LOG2E
    else:
        stats_ref, e_ref, dp_ref, chunk_ref = refs[-4:]
        flip_ref = bias_ref

    scale = head_width**-0.5 * LOG2E
    live = live_ref[0]
    key_live = lax.broadcasted_iota(jnp.int32, (BLOCK, BLOCK), 0) < live
    rows = live_rows(live)
    for j in range(GROUP_HEADS):
        mask = head_mask(j, head_width, HALF)
        head = group * GROUP_HEADS + j
        qm = window(q_ref, j) * mask
        gm = window(g_ref, j) * mask * rows
        x = dot(window(k_ref, j), qm, NT) * scale + skew(flip_ref[head : head + 1, : 2 * BLOCK])
        x = jnp.where(key_live, x, MASKED)
        m = reference_value(x)
        e = jnp.exp2(x - m)
        dp = dot(window(v_ref, j), gm, NT)
        e_ref[j] = e
        dp_ref[j] = dp
        stats_ref[0, j : j + 1, :] = m
        stats_ref[0, 4 + j : 5 + j, :] = jnp.sum(e, axis=0, keepdims=True)
        stats_ref[0, 8 + j : 9 + j, :] = jnp.sum(e * dp, axis=0, keepdims=True)
    stats_ref[0, 12:16, :] = jnp.zeros((4, BLOCK), jnp.float32)
    chunk_ref[:BLOCK, :] = g_ref[...]
    pack_rows(chunk_ref.at[BLOCK:PACKED, :], stats_ref[0])


def cross_kernel(
    head_width, group, live_ref, q_ref, g_ref, k_ref, v_ref, w_ref, *refs
):
    out_ref, dq_ref, dk_ref, dv_ref, lines_ref, rows_ref, dq_acc, dk_acc, dv_acc = refs[-9:]
    scale = head_width**-0.5 * LOG2E
    live = live_rows(live_ref[0])
    far_m, far_total, far_mixed = unpack_rows(g_ref.at[BLOCK:PACKED, :])
    heads = []
    for j in range(GROUP_HEADS):
        mask = head_mask(j, head_width, HALF)
        qm = window(q_ref, j, group) * mask
        gm = window(g_ref, j) * mask * live
        km = window(k_ref, j, group) * mask
        x = dot(km, qm, NT) * scale + skew(w_ref[group * GROUP_HEADS + j : group * GROUP_HEADS + j + 1, BLOCK:])
        m_far = far_m[j : j + 1]
        m = jnp.maximum(reference_value(x), m_far)
        e = jnp.exp2(x - m)
        dp = dot(window(v_ref, j, group), gm, NT)
        shrink = jnp.exp2(m_far - m)
        total = jnp.sum(e, axis=0, keepdims=True) + far_total[j : j + 1] * shrink
        mixed = jnp.sum(e * dp, axis=0, keepdims=True) + far_mixed[j : j + 1] * shrink
        inverse = 1.0 / total
        delta = mixed * inverse
        rows_ref[j : j + 1, :] = m
        rows_ref[4 + j : 5 + j, :] = inverse
        rows_ref[8 + j : 9 + j, :] = delta
        p = e * inverse
        ds = p * (dp - delta)
        put_lines(lines_ref, j, unskew(ds))
        heads.append((qm, gm, km, p.astype(HALF), ds.astype(HALF)))
    pair_products(heads, dq_acc, dk_acc, dv_acc)
    rows_ref[12:16, :] = jnp.zeros((4, BLOCK), jnp.float32)
    pack_rows(out_ref, rows_ref[...])
    scaling = head_width**-0.5
    dq_ref[...] = (dq_acc[...] * scaling).astype(HALF)
    dk_ref[...] = (dk_acc[...] * scaling).astype(HALF)
    dv_ref[...] = dv_acc[...].astype(HALF)


ROW_TILES = 3 * BLOCK // 128


def place(row, tile, parts):
    each = parts[2] // 128
    at = row * ROW_TILES + tile
    return at // each, slice(128 * (at % each), 128 * (at % each) + 128)


def spread_kernel(terms_ref, out_ref):
    total = terms_ref[0]
    for part in range(1, terms_ref.shape[0]):
        total = total + terms_ref[part]
    for part in range(out_ref.shape[0]):
        out_ref[part] = total


def gather_kernel(count, every_ref, _, out_ref):
    terms = every_ref.shape[0] // count
    shape_of_parts = (count,) + every_ref.shape[1:]
    totals = []
    for part in range(count):
        total = every_ref[part * terms]
        for term in range(1, terms):
            total = total + every_ref[part * terms + term]
        totals.append(total)
    for row in range(out_ref.shape[0]):
        for tile in range(ROW_TILES):
            part, lanes = place(row, tile, shape_of_parts)
            out_ref[row : row + 1, 128 * tile : 128 * tile + 128] = totals[part][:, lanes]


def own_parts(head, group, j, e_ref, dp_ref, near_ref, given):
    given_m, given_inverse, given_delta = given
    m_near = near_ref[group, j : j + 1, :]
    inverse_near = 1.0 / near_ref[group, 4 + j : 5 + j, :]
    inverse = given_inverse[j : j + 1]
    there = inverse > 0.0
    m = jnp.where(there, given_m[j : j + 1], m_near)
    ratio = jnp.exp2(m_near - m) * jnp.where(there, inverse, inverse_near)
    delta = jnp.where(there, given_delta[j : j + 1], near_ref[group, 8 + j : 9 + j, :] * inverse_near)
    p = e_ref[head] * ratio
    return p, p * (dp_ref[head] - delta)


def lanes_of(group):
    return slice(group * GROUP_LANES, (group + 1) * GROUP_LANES)


def table_kernel(groups, e_ref, dp_ref, near_ref, given_ref, cross_ref, table_ref, lines_ref):
    table_ref[...] = jnp.zeros_like(table_ref)
    for group in range(groups):
        given = unpack_rows(given_ref.at[:, lanes_of(group)])
        for j in range(GROUP_HEADS):
            _, ds = own_parts(group * GROUP_HEADS + j, group, j, e_ref, dp_ref, near_ref, given)
            put_lines(lines_ref.at[group : group + 1], j, unskew(ds))
        a, b = lined(lines_ref, group), lined(cross_ref, group)
        row = jnp.concatenate([a[:, :BLOCK], a[:, BLOCK:] + b[:, :BLOCK], b[:, BLOCK:]], axis=1)
        row = flipped(row)
        for j in range(GROUP_HEADS):
            for tile in range(ROW_TILES):
                part, lanes = place(group * GROUP_HEADS + j, tile, table_ref.shape)
                table_ref[part, :, lanes] = row[j : j + 1, 128 * tile : 128 * tile + 128]


def own_kernel(
    groups, head_width, live_ref, q_ref, g_ref, k_ref, e_ref, dp_ref, near_ref, given_ref, dqc_ref, dkc_ref, dvc_ref,
    dq_ref, dk_ref, dv_ref, dq_acc, dk_acc, dv_acc,
):
    live = live_rows(live_ref[0])

    def one_group(group):
        lanes = lanes_of(group)
        given = unpack_rows(given_ref.at[:, lanes])
        heads = []
        for j in range(GROUP_HEADS):
            mask = head_mask(j, head_width, HALF)
            qm = window(q_ref, j, group) * mask
            gm = window(g_ref, j, group) * mask * live
            km = window(k_ref, j, group) * mask
            p, ds = own_parts(group * GROUP_HEADS + j, group, j, e_ref, dp_ref, near_ref, given)
            heads.append((qm, gm, km, p.astype(HALF), ds.astype(HALF)))
        pair_products(heads, dq_acc, dk_acc, dv_acc)
        scaling = head_width**-0.5
        f32 = jnp.float32
        dq_ref[...] = (dq_acc[...] * scaling + dqc_ref[:, lanes].astype(f32)).astype(HALF)
        dk_ref[...] = (dk_acc[...] * scaling + dkc_ref[:, lanes].astype(f32)).astype(HALF)
        dv_ref[...] = (dv_acc[...] + dvc_ref[:, lanes].astype(f32)).astype(HALF)

    for group in range(groups):
        pl.when(pl.program_id(0) == group)(functools.partial(one_group, group))


def params(mebibytes=32):
    return pltpu.CompilerParams(vmem_limit_bytes=mebibytes * 1024 * 1024)


COST = pl.CostEstimate(flops=1024, bytes_accessed=1024, transcendentals=0)
LONG = pl.CostEstimate(flops=10**11, bytes_accessed=1024, transcendentals=0)


def shape(s, t=jnp.float32):
    return jax.ShapeDtypeStruct(s, t)


SMEM = pl.BlockSpec(memory_space=pltpu.SMEM)
ANY = pl.BlockSpec(memory_space=pl.ANY)
VMEM = pl.BlockSpec(memory_space=pltpu.VMEM)
ACCS = [pltpu.VMEM((BLOCK, GROUP_LANES), jnp.float32)] * 3
PACKED = BLOCK + 16
LINES = (1, 4, 8 * GROUP_HEADS, 128)


def whole_spec(s):
    return pl.BlockSpec(s, lambda i: (0,) * len(s))


def columns(first=0):
    return pl.BlockSpec((BLOCK, GROUP_LANES), lambda i: (0, first + i))


def stack(size, *rest, first=0):
    return pl.BlockSpec((size,) + rest, lambda i: (first + i,) + (0,) * len(rest))


def columns(first=0, rows=BLOCK):
    return pl.BlockSpec((rows, GROUP_LANES), lambda i: (0, first + i))


def stack(size, *rest, first=0):
    return pl.BlockSpec((size,) + rest, lambda i: (first + i,) + (0,) * len(rest))


def own_stats(head_width, group, live, q, g, k, v, bias, before):
    heads = bias.shape[0]
    groups = heads // GROUP_HEADS
    squares = stack(GROUP_HEADS, BLOCK, BLOCK, first=group)
    outs = [
        shape((groups, 16, BLOCK)),
        shape((heads, BLOCK, BLOCK)),
        shape((heads, BLOCK, BLOCK)),
        shape((PACKED, GROUP_LANES), HALF),
    ]
    out_specs = [stack(1, 16, BLOCK, first=group), squares, squares, whole_spec((PACKED, GROUP_LANES))]
    if not before:
        outs.append(shape(bias.shape))
        out_specs.append(whole_spec(bias.shape))
    return pl.pallas_call(
        functools.partial(own_stats_kernel, head_width, group),
        grid=(1,),
        in_specs=[SMEM] + [columns(group)] * 4 + [whole_spec(bias.shape)] + [ANY] * len(before),
        out_specs=out_specs,
        out_shape=outs,
        input_output_aliases={6 + i: i for i in range(len(before))},
        compiler_params=params(60),
        cost_estimate=COST,
        name=f"own_stats_{group}",
    )(live, q, g, k, v, bias, *before)


def cross(head_width, group, live, q, g, k, v, w, before):
    half = shape(q.shape, HALF)
    groups = q.shape[1] // GROUP_LANES
    return pl.pallas_call(
        functools.partial(cross_kernel, head_width, group),
        grid=(1,),
        in_specs=[SMEM] + [VMEM] * 5 + [ANY] * len(before),
        out_specs=[columns(group, 16), columns(group), columns(group), columns(group), stack(*LINES, first=group)],
        out_shape=[shape((16, q.shape[1]), HALF), half, half, half, shape((groups,) + LINES[1:])],
        scratch_shapes=[pltpu.VMEM((16, BLOCK), jnp.float32)] + ACCS,
        input_output_aliases={6 + i: i for i in range(len(before))},
        compiler_params=params(),
        cost_estimate=COST,
        name=f"cross_{group}",
    )(live, q, g, k, v, w, *before)


def table_sums(e, dp, near, given, lines, parts):
    groups = near.shape[0]
    return pl.pallas_call(
        functools.partial(table_kernel, groups),
        in_specs=[VMEM] * 5,
        out_shape=shape((parts, 1, -(-groups * GROUP_HEADS * ROW_TILES // parts) * 128)),
        scratch_shapes=[pltpu.VMEM(lines.shape, jnp.float32)],
        compiler_params=params(),
        cost_estimate=LONG,
        name="table_sums",
    )(e, dp, near, given, lines)


def own(head_width, live, q, g, k, e, dp, near, given, dqc, dkc, dvc):
    groups = near.shape[0]
    return pl.pallas_call(
        functools.partial(own_kernel, groups, head_width),
        grid=(groups,),
        in_specs=[SMEM] + [VMEM] * 10,
        out_specs=[columns()] * 3,
        out_shape=[shape(q.shape, HALF)] * 3,
        scratch_shapes=ACCS,
        compiler_params=params(),
        cost_estimate=LONG,
        name="own",
    )(live, q, g, k, e, dp, near, given, dqc, dkc, dvc)


def spread(terms, count):
    return pl.pallas_call(
        spread_kernel,
        out_shape=pltpu.HBM((count,) + terms.shape[1:], jnp.float32),
        out_specs=VMEM,
        compiler_params=params(),
        cost_estimate=COST,
        name="spread",
    )(terms)


def sum_over_devices(parts, inner, outer, heads, after):
    count = parts.shape[0]
    terms = lax.all_to_all(parts, inner, 0, 0)
    sums = spread(terms, count * lax.axis_size(outer))
    every = lax.all_to_all(sums, (inner, outer), 0, 0)
    return pl.pallas_call(
        functools.partial(gather_kernel, count),
        in_specs=[VMEM, ANY],
        out_shape=shape((heads, 3 * BLOCK)),
        compiler_params=params(),
        cost_estimate=COST,
        name="gather",
    )(every, pltpu.with_memory_space_constraint(after, pltpu.HBM))


def per_device(queries, keys, values, out_grad, lengths, rel_bias):
    frame_count, feature_width = queries.shape[1:]
    head_count = rel_bias.shape[0]
    head_width = feature_width // head_count
    groups = head_count // GROUP_HEADS
    live_own = lengths - lax.axis_index("tm") * BLOCK
    live_next = live_own - BLOCK
    q, k, v, g = (a.reshape(frame_count, feature_width) for a in (queries, keys, values, out_grad))

    q_next = shifted(q, "tm", -1)
    *before, chunk, w = own_stats(head_width, 0, live_own, q, g, k, v, rel_bias, ())
    chunks = [shifted(chunk, "tm", -1)]
    for group in range(1, groups):
        *before, chunk = own_stats(head_width, group, live_own, q, g, k, v, w, before)
        chunks.append(shifted(chunk, "tm", -1))
    near, e, dp = before
    results = ()
    for group in range(groups):
        results = cross(head_width, group, live_next, q_next, chunks[group], k, v, w, results)
    given, dq_cross, dkc, dvc, lines = results
    given = shifted(given, "tm", 1)
    dq_cross = shifted(dq_cross, "tm", 1)
    parts = lax.axis_size("dp")
    table = table_sums(e, dp, near, given, lines, parts)
    late = (pltpu.with_memory_space_constraint(a, pltpu.HBM) for a in (e, dp, near, given))
    dq, dk, dv = own(head_width, live_own, q, g, k, *late, dq_cross, dkc, dvc)
    bias_grad = sum_over_devices(table, "dp", "tm", head_count, dq)
    return tuple(a[None] for a in (dq, dk, dv)) + (bias_grad,)


def solution(mesh):
    block = P("dp", "tm", None)
    return jax.shard_map(
        per_device,
        mesh=mesh,
        in_specs=(block, block, block, block, P("dp"), P()),
        out_specs=(block, block, block, P()),
        check_vma=False,
    )
```

```python
import functools

import jax
import jax.numpy as jnp
import numpy as np
from jax import lax
from jax.experimental import pallas as pl
from jax.experimental.pallas import tpu as pltpu
from jax.sharding import PartitionSpec as P

BLOCK = 256
HALF = jnp.bfloat16
LOG2E = float(np.log2(np.e))
MASKED = -(2.0**30)
GROUP_HEADS = 4
GROUP_LANES = 384
WIDTH = 256
FIRST = (0, 0, 128, 128)

NT = (((1,), (1,)), ((), ()))
NN = (((1,), (0,)), ((), ()))
TN = (((0,), (0,)), ((), ()))


def dot(a, b, dims):
    return lax.dot_general(a, b, dims, preferred_element_type=jnp.float32)


def shifted(x, axis, by):
    count = lax.axis_size(axis)
    pairs = [(i, i + by) for i in range(count) if 0 <= i + by < count]
    return lax.ppermute(x, axis, pairs)


def head_mask(j, head_width, dtype):
    lane = lax.broadcasted_iota(jnp.int32, (1, WIDTH), 1) + FIRST[j]
    inside = (lane >= j * head_width) & (lane < (j + 1) * head_width)
    return jnp.where(inside, 1.0, 0.0).astype(dtype)


def skew(row):
    base = pltpu.roll(jnp.broadcast_to(row, (8, 2 * BLOCK)), 0, 1, stride=1, stride_axis=0)
    turns = [pltpu.roll(base, 8 * a, 1) if a else base for a in range(16)]
    near = [turn[:, BLOCK:] for turn in turns]
    far = [turn[:, BLOCK - 128 : 2 * BLOCK - 128] for turn in turns]
    return jnp.concatenate(near + far, axis=0)


def unskew(matrix):
    zeros = jnp.zeros((8, 128), jnp.float32)
    total = None
    for a in range(16):
        upper = matrix[8 * a : 8 * a + 8]
        lower = matrix[128 + 8 * a : 136 + 8 * a]
        part = jnp.concatenate(
            [zeros, lower[:, :128], upper[:, :128] + lower[:, 128:], upper[:, 128:]], axis=1
        )
        if a:
            part = pltpu.roll(part, 2 * BLOCK - 8 * a, 1)
        total = part if total is None else total + part
    return total


def flipped(rows):
    tiles = rows.shape[1] // 128
    a = lax.broadcasted_iota(jnp.int32, (128, 128), 0)
    b = lax.broadcasted_iota(jnp.int32, (128, 128), 1)
    swap = jnp.where(a + b == 127, 1.0, 0.0).astype(jnp.bfloat16)
    total = None
    for _ in range(3):
        piece = rows.astype(jnp.bfloat16)
        rows = rows - piece.astype(jnp.float32)
        moved = jnp.concatenate(
            [dot(piece[:, 128 * t : 128 * t + 128], swap, NN) for t in reversed(range(tiles))], axis=1
        )
        total = moved if total is None else total + moved
    return total


def window(ref, j, group=0):
    first = group * GROUP_LANES + FIRST[j]
    return ref[:BLOCK, first : first + WIDTH]


def live_rows(count):
    row = lax.broadcasted_iota(jnp.int32, (BLOCK, WIDTH), 0)
    return jnp.where(row < count, 1.0, 0.0).astype(HALF)


def put_lines(ref, j, lines):
    for tile in range(4):
        ref[0, tile, 8 * j : 8 * j + 8, :] = lines[:, 128 * tile : 128 * tile + 128]


def get_lines(ref, group, r):
    rows = pl.ds(r, GROUP_HEADS, stride=8)
    return jnp.concatenate([ref[group, tile, rows, :] for tile in range(4)], axis=1)


def lined(ref, group):
    total = get_lines(ref, group, 0)
    for r in range(1, 8):
        total = total + pltpu.roll(get_lines(ref, group, r), 2 * BLOCK - r, 1)
    return total


def pack_rows(ref, rows):
    high = rows.astype(HALF).astype(jnp.float32)
    low = rows - high
    main = jnp.concatenate([high[:12], low[4:8]], axis=0)
    side = jnp.concatenate([low[8:12, :128], low[8:12, 128:], jnp.zeros((8, 128), jnp.float32)], axis=0)
    ref[...] = jnp.concatenate([main, side], axis=1).astype(HALF)


def unpack_rows(ref):
    strip = ref[...].astype(jnp.float32)
    m = strip[:4, :BLOCK]
    total = strip[4:8, :BLOCK] + strip[12:16, :BLOCK]
    mixed = strip[8:12, :BLOCK] + jnp.concatenate([strip[:4, BLOCK:], strip[4:8, BLOCK:]], axis=1)
    return m, total, mixed


def reference_value(x):
    return jnp.max(x, axis=0, keepdims=True).astype(HALF).astype(jnp.float32)


def pair_products(heads, dq_acc, dk_acc, dv_acc):
    for pair in range(2):
        qm, gm, km, p, ds = zip(*heads[2 * pair : 2 * pair + 2])
        ps, dss = (jnp.concatenate(x, axis=1) for x in (p, ds))
        products = (
            (dv_acc, dot(ps, jnp.concatenate(gm, axis=0), NN)),
            (dk_acc, dot(dss, jnp.concatenate(qm, axis=0), NN)),
            (dq_acc, dot(jnp.concatenate(ds, axis=0), jnp.concatenate(km, axis=0), TN)),
        )
        for ref, value in products:
            if pair == 0:
                ref[:, :WIDTH] = value
            else:
                ref[:, 128:WIDTH] += value[:, :128]
                ref[:, WIDTH:] = value[:, 128:]


def own_stats_kernel(
    head_width, group, live_ref, q_ref, g_ref, k_ref, v_ref, bias_ref, *refs
):
    if group == 0:
        stats_ref, e_ref, dp_ref, chunk_ref, flip_ref = refs
        flip_ref[...] = flipped(bias_ref[...]) * LOG2E
    else:
        stats_ref, e_ref, dp_ref, chunk_ref = refs[-4:]
        flip_ref = bias_ref

    scale = head_width**-0.5 * LOG2E
    live = live_ref[0]
    key_live = lax.broadcasted_iota(jnp.int32, (BLOCK, BLOCK), 0) < live
    rows = live_rows(live)
    for j in range(GROUP_HEADS):
        mask = head_mask(j, head_width, HALF)
        head = group * GROUP_HEADS + j
        qm = window(q_ref, j) * mask
        gm = window(g_ref, j) * mask * rows
        x = dot(window(k_ref, j), qm, NT) * scale + skew(flip_ref[head : head + 1, : 2 * BLOCK])
        x = jnp.where(key_live, x, MASKED)
        m = reference_value(x)
        e = jnp.exp2(x - m)
        dp = dot(window(v_ref, j), gm, NT)
        e_ref[j] = e
        dp_ref[j] = dp
        stats_ref[0, j : j + 1, :] = m
        stats_ref[0, 4 + j : 5 + j, :] = jnp.sum(e, axis=0, keepdims=True)
        stats_ref[0, 8 + j : 9 + j, :] = jnp.sum(e * dp, axis=0, keepdims=True)
    stats_ref[0, 12:16, :] = jnp.zeros((4, BLOCK), jnp.float32)
    chunk_ref[:BLOCK, :] = g_ref[...]
    pack_rows(chunk_ref.at[BLOCK:PACKED, :], stats_ref[0])


def cross_kernel(
    head_width, group, live_ref, q_ref, g_ref, k_ref, v_ref, w_ref, *refs
):
    out_ref, dq_ref, dk_ref, dv_ref, lines_ref, rows_ref, dq_acc, dk_acc, dv_acc = refs[-9:]
    scale = head_width**-0.5 * LOG2E
    live = live_rows(live_ref[0])
    far_m, far_total, far_mixed = unpack_rows(g_ref.at[BLOCK:PACKED, :])
    heads = []
    for j in range(GROUP_HEADS):
        mask = head_mask(j, head_width, HALF)
        qm = window(q_ref, j, group) * mask
        gm = window(g_ref, j) * mask * live
        km = window(k_ref, j, group) * mask
        x = dot(km, qm, NT) * scale + skew(w_ref[group * GROUP_HEADS + j : group * GROUP_HEADS + j + 1, BLOCK:])
        m_far = far_m[j : j + 1]
        m = jnp.maximum(reference_value(x), m_far)
        e = jnp.exp2(x - m)
        dp = dot(window(v_ref, j, group), gm, NT)
        shrink = jnp.exp2(m_far - m)
        total = jnp.sum(e, axis=0, keepdims=True) + far_total[j : j + 1] * shrink
        mixed = jnp.sum(e * dp, axis=0, keepdims=True) + far_mixed[j : j + 1] * shrink
        inverse = 1.0 / total
        delta = mixed * inverse
        rows_ref[j : j + 1, :] = m
        rows_ref[4 + j : 5 + j, :] = inverse
        rows_ref[8 + j : 9 + j, :] = delta
        p = e * inverse
        ds = p * (dp - delta)
        put_lines(lines_ref, j, unskew(ds))
        heads.append((qm, gm, km, p.astype(HALF), ds.astype(HALF)))
    pair_products(heads, dq_acc, dk_acc, dv_acc)
    rows_ref[12:16, :] = jnp.zeros((4, BLOCK), jnp.float32)
    pack_rows(out_ref, rows_ref[...])
    scaling = head_width**-0.5
    dq_ref[...] = (dq_acc[...] * scaling).astype(HALF)
    dk_ref[...] = (dk_acc[...] * scaling).astype(HALF)
    dv_ref[...] = dv_acc[...].astype(HALF)


ROW_TILES = 3 * BLOCK // 128


def place(row, tile, parts):
    each = parts[2] // 128
    at = row * ROW_TILES + tile
    return at // each, slice(128 * (at % each), 128 * (at % each) + 128)


def spread_kernel(terms_ref, out_ref):
    total = terms_ref[0]
    for part in range(1, terms_ref.shape[0]):
        total = total + terms_ref[part]
    for part in range(out_ref.shape[0]):
        out_ref[part] = total


def gather_kernel(count, every_ref, _, out_ref):
    each = every_ref.shape[2] // 128

    def one_part(part):
        total = every_ref[0]
        for term in range(1, every_ref.shape[0]):
            total = total + every_ref[term]
        for tile in range(min(each, out_ref.shape[0] * ROW_TILES - part * each)):
            row, lane = divmod(part * each + tile, ROW_TILES)
            out_ref[row : row + 1, 128 * lane : 128 * lane + 128] = total[:, 128 * tile : 128 * tile + 128]

    for part in range(count):
        pl.when(pl.program_id(0) == part)(functools.partial(one_part, part))


def final_factors(group, j, near_ref, given):
    given_m, given_inverse, given_delta = given
    m_near = near_ref[group, j : j + 1, :]
    inverse_near = 1.0 / near_ref[group, 4 + j : 5 + j, :]
    inverse = given_inverse[j : j + 1]
    there = inverse > 0.0
    m = jnp.where(there, given_m[j : j + 1], m_near)
    ratio = jnp.exp2(m_near - m) * jnp.where(there, inverse, inverse_near)
    delta = jnp.where(there, given_delta[j : j + 1], near_ref[group, 8 + j : 9 + j, :] * inverse_near)
    return ratio, delta


def lanes_of(group):
    return slice(group * GROUP_LANES, (group + 1) * GROUP_LANES)


def table_kernel(groups, e_ref, dp_ref, near_ref, given_ref, cross_ref, table_ref, factors_ref, lines_ref):
    table_ref[...] = jnp.zeros_like(table_ref)
    for group in range(groups):
        given = unpack_rows(given_ref.at[:, lanes_of(group)])
        for j in range(GROUP_HEADS):
            head = group * GROUP_HEADS + j
            ratio, delta = final_factors(group, j, near_ref, given)
            factors_ref[group, j : j + 1, :] = ratio
            factors_ref[group, 4 + j : 5 + j, :] = delta
            ds = e_ref[head] * ratio * (dp_ref[head] - delta)
            put_lines(lines_ref.at[group : group + 1], j, unskew(ds))
        a, b = lined(lines_ref, group), lined(cross_ref, group)
        row = jnp.concatenate([a[:, :BLOCK], a[:, BLOCK:] + b[:, :BLOCK], b[:, BLOCK:]], axis=1)
        row = flipped(row)
        for j in range(GROUP_HEADS):
            for tile in range(ROW_TILES):
                part, lanes = place(group * GROUP_HEADS + j, tile, table_ref.shape)
                table_ref[part, :, lanes] = row[j : j + 1, 128 * tile : 128 * tile + 128]


def own_kernel(
    groups, head_width, live_ref, q_ref, g_ref, k_ref, e_ref, dp_ref, factors_ref, dqc_ref, dkc_ref, dvc_ref,
    dq_ref, dk_ref, dv_ref, dq_acc, dk_acc, dv_acc,
):
    live = live_rows(live_ref[0])

    def one_group(group):
        lanes = lanes_of(group)
        heads = []
        for j in range(GROUP_HEADS):
            mask = head_mask(j, head_width, HALF)
            qm = window(q_ref, j, group) * mask
            gm = window(g_ref, j, group) * mask * live
            km = window(k_ref, j, group) * mask
            head = group * GROUP_HEADS + j
            p = e_ref[head] * factors_ref[group, j : j + 1, :]
            ds = p * (dp_ref[head] - factors_ref[group, 4 + j : 5 + j, :])
            heads.append((qm, gm, km, p.astype(HALF), ds.astype(HALF)))
        pair_products(heads, dq_acc, dk_acc, dv_acc)
        scaling = head_width**-0.5
        f32 = jnp.float32
        dq_ref[...] = (dq_acc[...] * scaling + dqc_ref[:, lanes].astype(f32)).astype(HALF)
        dk_ref[...] = (dk_acc[...] * scaling + dkc_ref[:, lanes].astype(f32)).astype(HALF)
        dv_ref[...] = (dv_acc[...] + dvc_ref[:, lanes].astype(f32)).astype(HALF)

    for group in range(groups):
        pl.when(pl.program_id(0) == group)(functools.partial(one_group, group))


def params(mebibytes=32):
    return pltpu.CompilerParams(vmem_limit_bytes=mebibytes * 1024 * 1024)


COST = pl.CostEstimate(flops=1024, bytes_accessed=1024, transcendentals=0)
LONG = pl.CostEstimate(flops=10**11, bytes_accessed=1024, transcendentals=0)


def shape(s, t=jnp.float32):
    return jax.ShapeDtypeStruct(s, t)


SMEM = pl.BlockSpec(memory_space=pltpu.SMEM)
ANY = pl.BlockSpec(memory_space=pl.ANY)
VMEM = pl.BlockSpec(memory_space=pltpu.VMEM)
ACCS = [pltpu.VMEM((BLOCK, GROUP_LANES), jnp.float32)] * 3
PACKED = BLOCK + 16
LINES = (1, 4, 8 * GROUP_HEADS, 128)


def whole_spec(s):
    return pl.BlockSpec(s, lambda i: (0,) * len(s))


def columns(first=0):
    return pl.BlockSpec((BLOCK, GROUP_LANES), lambda i: (0, first + i))


def stack(size, *rest, first=0):
    return pl.BlockSpec((size,) + rest, lambda i: (first + i,) + (0,) * len(rest))


def columns(first=0, rows=BLOCK):
    return pl.BlockSpec((rows, GROUP_LANES), lambda i: (0, first + i))


def stack(size, *rest, first=0):
    return pl.BlockSpec((size,) + rest, lambda i: (first + i,) + (0,) * len(rest))


def own_stats(head_width, group, live, q, g, k, v, bias, before):
    heads = bias.shape[0]
    groups = heads // GROUP_HEADS
    squares = stack(GROUP_HEADS, BLOCK, BLOCK, first=group)
    outs = [
        shape((groups, 16, BLOCK)),
        shape((heads, BLOCK, BLOCK)),
        shape((heads, BLOCK, BLOCK)),
        shape((PACKED, GROUP_LANES), HALF),
    ]
    out_specs = [stack(1, 16, BLOCK, first=group), squares, squares, whole_spec((PACKED, GROUP_LANES))]
    if not before:
        outs.append(shape(bias.shape))
        out_specs.append(whole_spec(bias.shape))
    return pl.pallas_call(
        functools.partial(own_stats_kernel, head_width, group),
        grid=(1,),
        in_specs=[SMEM] + [columns(group)] * 4 + [whole_spec(bias.shape)] + [ANY] * len(before),
        out_specs=out_specs,
        out_shape=outs,
        input_output_aliases={6 + i: i for i in range(len(before))},
        compiler_params=params(60),
        cost_estimate=COST,
        name=f"own_stats_{group}",
    )(live, q, g, k, v, bias, *before)


def cross(head_width, group, live, q, g, k, v, w, before):
    half = shape(q.shape, HALF)
    groups = q.shape[1] // GROUP_LANES
    return pl.pallas_call(
        functools.partial(cross_kernel, head_width, group),
        grid=(1,),
        in_specs=[SMEM] + [VMEM] * 5 + [ANY] * len(before),
        out_specs=[columns(group, 16), columns(group), columns(group), columns(group), stack(*LINES, first=group)],
        out_shape=[shape((16, q.shape[1]), HALF), half, half, half, shape((groups,) + LINES[1:])],
        scratch_shapes=[pltpu.VMEM((16, BLOCK), jnp.float32)] + ACCS,
        input_output_aliases={6 + i: i for i in range(len(before))},
        compiler_params=params(),
        cost_estimate=COST,
        name=f"cross_{group}",
    )(live, q, g, k, v, w, *before)


def table_sums(e, dp, near, given, lines, parts):
    groups = near.shape[0]
    return pl.pallas_call(
        functools.partial(table_kernel, groups),
        in_specs=[VMEM] * 5,
        out_specs=[VMEM, VMEM],
        out_shape=[
            shape((parts, 1, -(-groups * GROUP_HEADS * ROW_TILES // parts) * 128)),
            pltpu.HBM((groups, 2 * GROUP_HEADS, BLOCK), jnp.float32),
        ],
        scratch_shapes=[pltpu.VMEM(lines.shape, jnp.float32)],
        compiler_params=params(),
        cost_estimate=LONG,
        name="table_sums",
    )(e, dp, near, given, lines)


def own(head_width, live, q, g, k, e, dp, factors, dqc, dkc, dvc):
    groups = factors.shape[0]
    return pl.pallas_call(
        functools.partial(own_kernel, groups, head_width),
        grid=(groups,),
        in_specs=[SMEM] + [VMEM] * 9,
        out_specs=[columns()] * 3,
        out_shape=[shape(q.shape, HALF)] * 3,
        scratch_shapes=ACCS,
        compiler_params=params(),
        cost_estimate=LONG,
        name="own",
    )(live, q, g, k, e, dp, factors, dqc, dkc, dvc)


def spread(terms, count):
    return pl.pallas_call(
        spread_kernel,
        out_shape=pltpu.HBM((count,) + terms.shape[1:], jnp.float32),
        out_specs=VMEM,
        compiler_params=params(),
        cost_estimate=COST,
        name="spread",
    )(terms)


def sum_over_devices(parts, inner, outer, heads, after):
    count = parts.shape[0]
    terms = lax.all_to_all(parts, inner, 0, 0)
    sums = spread(terms, count * lax.axis_size(outer))
    every = lax.all_to_all(sums, (inner, outer), 0, 0)
    return pl.pallas_call(
        functools.partial(gather_kernel, count),
        grid=(count,),
        in_specs=[stack(every.shape[0] // count, *every.shape[1:]), ANY],
        out_specs=whole_spec((heads, 3 * BLOCK)),
        out_shape=shape((heads, 3 * BLOCK)),
        compiler_params=params(),
        cost_estimate=COST,
        name="gather",
    )(every, pltpu.with_memory_space_constraint(after, pltpu.HBM))


def per_device(queries, keys, values, out_grad, lengths, rel_bias):
    frame_count, feature_width = queries.shape[1:]
    head_count = rel_bias.shape[0]
    head_width = feature_width // head_count
    groups = head_count // GROUP_HEADS
    live_own = lengths - lax.axis_index("tm") * BLOCK
    live_next = live_own - BLOCK
    q, k, v, g = (a.reshape(frame_count, feature_width) for a in (queries, keys, values, out_grad))

    q_next = shifted(q, "tm", -1)
    *before, chunk, w = own_stats(head_width, 0, live_own, q, g, k, v, rel_bias, ())
    chunks = [shifted(chunk, "tm", -1)]
    for group in range(1, groups):
        *before, chunk = own_stats(head_width, group, live_own, q, g, k, v, w, before)
        chunks.append(shifted(chunk, "tm", -1))
    near, e, dp = before
    results = ()
    for group in range(groups):
        results = cross(head_width, group, live_next, q_next, chunks[group], k, v, w, results)
    given, dq_cross, dkc, dvc, lines = results
    given = shifted(given, "tm", 1)
    dq_cross = shifted(dq_cross, "tm", 1)
    parts = lax.axis_size("dp")
    table, factors = table_sums(e, dp, near, given, lines, parts)
    late = (pltpu.with_memory_space_constraint(a, pltpu.HBM) for a in (e, dp, factors))
    dq, dk, dv = own(head_width, live_own, q, g, k, *late, dq_cross, dkc, dvc)
    bias_grad = sum_over_devices(table, "dp", "tm", head_count, dq)
    return tuple(a[None] for a in (dq, dk, dv)) + (bias_grad,)


def solution(mesh):
    block = P("dp", "tm", None)
    return jax.shard_map(
        per_device,
        mesh=mesh,
        in_specs=(block, block, block, block, P("dp"), P()),
        out_specs=(block, block, block, P()),
        check_vma=False,
    )
```

```python
import functools

import jax
import jax.numpy as jnp
import numpy as np
from jax import lax
from jax.experimental import pallas as pl
from jax.experimental.pallas import tpu as pltpu
from jax.sharding import PartitionSpec as P

BLOCK = 256
HALF = jnp.bfloat16
LOG2E = float(np.log2(np.e))
MASKED = -(2.0**30)
GROUP_HEADS = 4
GROUP_LANES = 384
WIDTH = 256
FIRST = (0, 0, 128, 128)

NT = (((1,), (1,)), ((), ()))
NN = (((1,), (0,)), ((), ()))
TN = (((0,), (0,)), ((), ()))


def dot(a, b, dims):
    return lax.dot_general(a, b, dims, preferred_element_type=jnp.float32)


def shifted(x, axis, by):
    count = lax.axis_size(axis)
    pairs = [(i, i + by) for i in range(count) if 0 <= i + by < count]
    return lax.ppermute(x, axis, pairs)


def head_mask(j, head_width, dtype):
    lane = lax.broadcasted_iota(jnp.int32, (1, WIDTH), 1) + FIRST[j]
    inside = (lane >= j * head_width) & (lane < (j + 1) * head_width)
    return jnp.where(inside, 1.0, 0.0).astype(dtype)


def skew(row):
    base = pltpu.roll(jnp.broadcast_to(row, (8, 2 * BLOCK)), 0, 1, stride=1, stride_axis=0)
    turns = [pltpu.roll(base, 8 * a, 1) if a else base for a in range(16)]
    near = [turn[:, BLOCK:] for turn in turns]
    far = [turn[:, BLOCK - 128 : 2 * BLOCK - 128] for turn in turns]
    return jnp.concatenate(near + far, axis=0)


def unskew(matrix):
    zeros = jnp.zeros((8, 128), jnp.float32)
    total = None
    for a in range(16):
        upper = matrix[8 * a : 8 * a + 8]
        lower = matrix[128 + 8 * a : 136 + 8 * a]
        part = jnp.concatenate(
            [zeros, lower[:, :128], upper[:, :128] + lower[:, 128:], upper[:, 128:]], axis=1
        )
        if a:
            part = pltpu.roll(part, 2 * BLOCK - 8 * a, 1)
        total = part if total is None else total + part
    return total


def flipped(rows):
    tiles = rows.shape[1] // 128
    a = lax.broadcasted_iota(jnp.int32, (128, 128), 0)
    b = lax.broadcasted_iota(jnp.int32, (128, 128), 1)
    swap = jnp.where(a + b == 127, 1.0, 0.0).astype(jnp.bfloat16)
    total = None
    for _ in range(3):
        piece = rows.astype(jnp.bfloat16)
        rows = rows - piece.astype(jnp.float32)
        moved = jnp.concatenate(
            [dot(piece[:, 128 * t : 128 * t + 128], swap, NN) for t in reversed(range(tiles))], axis=1
        )
        total = moved if total is None else total + moved
    return total


def window(ref, j, group=0):
    first = group * GROUP_LANES + FIRST[j]
    return ref[:BLOCK, first : first + WIDTH]


def live_rows(count):
    row = lax.broadcasted_iota(jnp.int32, (BLOCK, WIDTH), 0)
    return jnp.where(row < count, 1.0, 0.0).astype(HALF)


def put_lines(ref, j, lines):
    for tile in range(4):
        ref[0, tile, 8 * j : 8 * j + 8, :] = lines[:, 128 * tile : 128 * tile + 128]


def get_lines(ref, group, r):
    rows = pl.ds(r, GROUP_HEADS, stride=8)
    return jnp.concatenate([ref[group, tile, rows, :] for tile in range(4)], axis=1)


def lined(ref, group):
    total = get_lines(ref, group, 0)
    for r in range(1, 8):
        total = total + pltpu.roll(get_lines(ref, group, r), 2 * BLOCK - r, 1)
    return total


def pack_rows(ref, rows):
    high = rows.astype(HALF).astype(jnp.float32)
    low = rows - high
    main = jnp.concatenate([high[:12], low[4:8]], axis=0)
    side = jnp.concatenate([low[8:12, :128], low[8:12, 128:], jnp.zeros((8, 128), jnp.float32)], axis=0)
    ref[...] = jnp.concatenate([main, side], axis=1).astype(HALF)


def unpack_rows(ref):
    strip = ref[...].astype(jnp.float32)
    m = strip[:4, :BLOCK]
    total = strip[4:8, :BLOCK] + strip[12:16, :BLOCK]
    mixed = strip[8:12, :BLOCK] + jnp.concatenate([strip[:4, BLOCK:], strip[4:8, BLOCK:]], axis=1)
    return m, total, mixed


def reference_value(x):
    return jnp.max(x, axis=0, keepdims=True).astype(HALF).astype(jnp.float32)


def pair_products(heads, dq_acc, dk_acc, dv_acc):
    for pair in range(2):
        qm, gm, km, p, ds = zip(*heads[2 * pair : 2 * pair + 2])
        ps, dss = (jnp.concatenate(x, axis=1) for x in (p, ds))
        products = (
            (dv_acc, dot(ps, jnp.concatenate(gm, axis=0), NN)),
            (dk_acc, dot(dss, jnp.concatenate(qm, axis=0), NN)),
            (dq_acc, dot(jnp.concatenate(ds, axis=0), jnp.concatenate(km, axis=0), TN)),
        )
        for ref, value in products:
            if pair == 0:
                ref[:, :WIDTH] = value
            else:
                ref[:, 128:WIDTH] += value[:, :128]
                ref[:, WIDTH:] = value[:, 128:]


def own_stats_kernel(
    head_width, group, live_ref, q_ref, g_ref, k_ref, v_ref, bias_ref, *refs
):
    if group == 0:
        stats_ref, e_ref, dp_ref, chunk_ref, flip_ref = refs
        flip_ref[...] = flipped(bias_ref[...]) * LOG2E
    else:
        stats_ref, e_ref, dp_ref, chunk_ref = refs[-4:]
        flip_ref = bias_ref

    scale = head_width**-0.5 * LOG2E
    live = live_ref[0]
    key_live = lax.broadcasted_iota(jnp.int32, (BLOCK, BLOCK), 0) < live
    rows = live_rows(live)
    for j in range(GROUP_HEADS):
        mask = head_mask(j, head_width, HALF)
        head = group * GROUP_HEADS + j
        qm = window(q_ref, j) * mask
        gm = window(g_ref, j) * mask * rows
        x = dot(window(k_ref, j), qm, NT) * scale + skew(flip_ref[head : head + 1, : 2 * BLOCK])
        x = jnp.where(key_live, x, MASKED)
        m = reference_value(x)
        e = jnp.exp2(x - m)
        dp = dot(window(v_ref, j), gm, NT)
        e_ref[j] = e
        dp_ref[j] = dp
        stats_ref[0, j : j + 1, :] = m
        stats_ref[0, 4 + j : 5 + j, :] = jnp.sum(e, axis=0, keepdims=True)
        stats_ref[0, 8 + j : 9 + j, :] = jnp.sum(e * dp, axis=0, keepdims=True)
    stats_ref[0, 12:16, :] = jnp.zeros((4, BLOCK), jnp.float32)
    chunk_ref[:BLOCK, :] = g_ref[...]
    pack_rows(chunk_ref.at[BLOCK:PACKED, :], stats_ref[0])


def cross_kernel(
    head_width, group, live_ref, q_ref, g_ref, k_ref, v_ref, w_ref, *refs
):
    out_ref, dq_ref, dk_ref, dv_ref, lines_ref, rows_ref, dq_acc, dk_acc, dv_acc = refs[-9:]
    scale = head_width**-0.5 * LOG2E
    live = live_rows(live_ref[0])
    far_m, far_total, far_mixed = unpack_rows(g_ref.at[BLOCK:PACKED, :])
    heads = []
    for j in range(GROUP_HEADS):
        mask = head_mask(j, head_width, HALF)
        qm = window(q_ref, j, group) * mask
        gm = window(g_ref, j) * mask * live
        km = window(k_ref, j, group) * mask
        x = dot(km, qm, NT) * scale + skew(w_ref[group * GROUP_HEADS + j : group * GROUP_HEADS + j + 1, BLOCK:])
        m_far = far_m[j : j + 1]
        m = jnp.maximum(reference_value(x), m_far)
        e = jnp.exp2(x - m)
        dp = dot(window(v_ref, j, group), gm, NT)
        shrink = jnp.exp2(m_far - m)
        total = jnp.sum(e, axis=0, keepdims=True) + far_total[j : j + 1] * shrink
        mixed = jnp.sum(e * dp, axis=0, keepdims=True) + far_mixed[j : j + 1] * shrink
        inverse = 1.0 / total
        delta = mixed * inverse
        rows_ref[j : j + 1, :] = m
        rows_ref[4 + j : 5 + j, :] = inverse
        rows_ref[8 + j : 9 + j, :] = delta
        p = e * inverse
        ds = p * (dp - delta)
        put_lines(lines_ref, j, unskew(ds))
        heads.append((qm, gm, km, p.astype(HALF), ds.astype(HALF)))
    pair_products(heads, dq_acc, dk_acc, dv_acc)
    rows_ref[12:16, :] = jnp.zeros((4, BLOCK), jnp.float32)
    pack_rows(out_ref, rows_ref[...])
    scaling = head_width**-0.5
    dq_ref[...] = (dq_acc[...] * scaling).astype(HALF)
    dk_ref[...] = (dk_acc[...] * scaling).astype(HALF)
    dv_ref[...] = dv_acc[...].astype(HALF)


ROW_TILES = 3 * BLOCK // 128


def place(row, tile, parts):
    each = parts[2] // 128
    at = row * ROW_TILES + tile
    return at // each, slice(128 * (at % each), 128 * (at % each) + 128)


def spread_kernel(terms_ref, out_ref):
    total = terms_ref[0]
    for part in range(1, terms_ref.shape[0]):
        total = total + terms_ref[part]
    for part in range(out_ref.shape[0]):
        out_ref[part] = total


def gather_kernel(count, every_ref, _, out_ref):
    terms = every_ref.shape[0] // count
    shape_of_parts = (count,) + every_ref.shape[1:]
    totals = []
    for part in range(count):
        total = every_ref[part * terms]
        for term in range(1, terms):
            total = total + every_ref[part * terms + term]
        totals.append(total)
    for row in range(out_ref.shape[0]):
        for tile in range(ROW_TILES):
            part, lanes = place(row, tile, shape_of_parts)
            out_ref[row : row + 1, 128 * tile : 128 * tile + 128] = totals[part][:, lanes]


def own_parts(head, group, j, e_ref, dp_ref, near_ref, given):
    given_m, given_inverse, given_delta = given
    m_near = near_ref[group, j : j + 1, :]
    inverse_near = 1.0 / near_ref[group, 4 + j : 5 + j, :]
    inverse = given_inverse[j : j + 1]
    there = inverse > 0.0
    m = jnp.where(there, given_m[j : j + 1], m_near)
    ratio = jnp.exp2(m_near - m) * jnp.where(there, inverse, inverse_near)
    delta = jnp.where(there, given_delta[j : j + 1], near_ref[group, 8 + j : 9 + j, :] * inverse_near)
    p = e_ref[head] * ratio
    return p, p * (dp_ref[head] - delta)


def lanes_of(group):
    return slice(group * GROUP_LANES, (group + 1) * GROUP_LANES)


def table_kernel(groups, e_ref, dp_ref, near_ref, given_ref, cross_ref, table_ref, lines_ref):
    table_ref[...] = jnp.zeros_like(table_ref)
    for group in range(groups):
        given = unpack_rows(given_ref.at[:, lanes_of(group)])
        for j in range(GROUP_HEADS):
            _, ds = own_parts(group * GROUP_HEADS + j, group, j, e_ref, dp_ref, near_ref, given)
            put_lines(lines_ref.at[group : group + 1], j, unskew(ds))
        a, b = lined(lines_ref, group), lined(cross_ref, group)
        row = jnp.concatenate([a[:, :BLOCK], a[:, BLOCK:] + b[:, :BLOCK], b[:, BLOCK:]], axis=1)
        row = flipped(row)
        for j in range(GROUP_HEADS):
            for tile in range(ROW_TILES):
                part, lanes = place(group * GROUP_HEADS + j, tile, table_ref.shape)
                table_ref[part, :, lanes] = row[j : j + 1, 128 * tile : 128 * tile + 128]


def own_kernel(
    groups, head_width, live_ref, q_ref, g_ref, k_ref, e_ref, dp_ref, near_ref, given_ref, dqc_ref, dkc_ref, dvc_ref,
    dq_ref, dk_ref, dv_ref, dq_acc, dk_acc, dv_acc,
):
    live = live_rows(live_ref[0])

    def one_group(group):
        lanes = lanes_of(group)
        given = unpack_rows(given_ref.at[:, lanes])
        heads = []
        for j in range(GROUP_HEADS):
            mask = head_mask(j, head_width, HALF)
            qm = window(q_ref, j, group) * mask
            gm = window(g_ref, j, group) * mask * live
            km = window(k_ref, j, group) * mask
            p, ds = own_parts(group * GROUP_HEADS + j, group, j, e_ref, dp_ref, near_ref, given)
            heads.append((qm, gm, km, p.astype(HALF), ds.astype(HALF)))
        pair_products(heads, dq_acc, dk_acc, dv_acc)
        scaling = head_width**-0.5
        f32 = jnp.float32
        dq_ref[...] = (dq_acc[...] * scaling + dqc_ref[:, lanes].astype(f32)).astype(HALF)
        dk_ref[...] = (dk_acc[...] * scaling + dkc_ref[:, lanes].astype(f32)).astype(HALF)
        dv_ref[...] = (dv_acc[...] + dvc_ref[:, lanes].astype(f32)).astype(HALF)

    for group in range(groups):
        pl.when(pl.program_id(0) == group)(functools.partial(one_group, group))


def params(mebibytes=32):
    return pltpu.CompilerParams(vmem_limit_bytes=mebibytes * 1024 * 1024)


COST = pl.CostEstimate(flops=1024, bytes_accessed=1024, transcendentals=0)
LONG = pl.CostEstimate(flops=10**11, bytes_accessed=1024, transcendentals=0)


def shape(s, t=jnp.float32):
    return jax.ShapeDtypeStruct(s, t)


SMEM = pl.BlockSpec(memory_space=pltpu.SMEM)
ANY = pl.BlockSpec(memory_space=pl.ANY)
VMEM = pl.BlockSpec(memory_space=pltpu.VMEM)
ACCS = [pltpu.VMEM((BLOCK, GROUP_LANES), jnp.float32)] * 3
PACKED = BLOCK + 16
LINES = (1, 4, 64, 128)


def whole_spec(s):
    return pl.BlockSpec(s, lambda i: (0,) * len(s))


def columns(first=0):
    return pl.BlockSpec((BLOCK, GROUP_LANES), lambda i: (0, first + i))


def stack(size, *rest, first=0):
    return pl.BlockSpec((size,) + rest, lambda i: (first + i,) + (0,) * len(rest))


def columns(first=0, rows=BLOCK):
    return pl.BlockSpec((rows, GROUP_LANES), lambda i: (0, first + i))


def stack(size, *rest, first=0):
    return pl.BlockSpec((size,) + rest, lambda i: (first + i,) + (0,) * len(rest))


def own_stats(head_width, group, live, q, g, k, v, bias, before):
    heads = bias.shape[0]
    groups = heads // GROUP_HEADS
    squares = stack(GROUP_HEADS, BLOCK, BLOCK, first=group)
    outs = [
        shape((groups, 16, BLOCK)),
        shape((heads, BLOCK, BLOCK)),
        shape((heads, BLOCK, BLOCK)),
        shape((PACKED, GROUP_LANES), HALF),
    ]
    out_specs = [stack(1, 16, BLOCK, first=group), squares, squares, whole_spec((PACKED, GROUP_LANES))]
    if not before:
        outs.append(shape(bias.shape))
        out_specs.append(whole_spec(bias.shape))
    return pl.pallas_call(
        functools.partial(own_stats_kernel, head_width, group),
        grid=(1,),
        in_specs=[SMEM] + [columns(group)] * 4 + [whole_spec(bias.shape)] + [ANY] * len(before),
        out_specs=out_specs,
        out_shape=outs,
        input_output_aliases={6 + i: i for i in range(len(before))},
        compiler_params=params(60),
        cost_estimate=COST,
        name=f"own_stats_{group}",
    )(live, q, g, k, v, bias, *before)


def cross(head_width, group, live, q, g, k, v, w, before):
    half = shape(q.shape, HALF)
    groups = q.shape[1] // GROUP_LANES
    return pl.pallas_call(
        functools.partial(cross_kernel, head_width, group),
        grid=(1,),
        in_specs=[SMEM] + [VMEM] * 5 + [ANY] * len(before),
        out_specs=[columns(group, 16), columns(group), columns(group), columns(group), stack(*LINES, first=group)],
        out_shape=[shape((16, q.shape[1]), HALF), half, half, half, shape((groups,) + LINES[1:])],
        scratch_shapes=[pltpu.VMEM((16, BLOCK), jnp.float32)] + ACCS,
        input_output_aliases={6 + i: i for i in range(len(before))},
        compiler_params=params(),
        cost_estimate=COST,
        name=f"cross_{group}",
    )(live, q, g, k, v, w, *before)


def table_sums(e, dp, near, given, lines, parts):
    groups = near.shape[0]
    return pl.pallas_call(
        functools.partial(table_kernel, groups),
        in_specs=[VMEM] * 5,
        out_shape=shape((parts, 1, -(-groups * GROUP_HEADS * ROW_TILES // parts) * 128)),
        scratch_shapes=[pltpu.VMEM(lines.shape, jnp.float32)],
        compiler_params=params(),
        cost_estimate=LONG,
        name="table_sums",
    )(e, dp, near, given, lines)


def own(head_width, live, q, g, k, e, dp, near, given, dqc, dkc, dvc):
    groups = near.shape[0]
    return pl.pallas_call(
        functools.partial(own_kernel, groups, head_width),
        grid=(groups,),
        in_specs=[SMEM] + [VMEM] * 10,
        out_specs=[columns()] * 3,
        out_shape=[shape(q.shape, HALF)] * 3,
        scratch_shapes=ACCS,
        compiler_params=params(),
        cost_estimate=LONG,
        name="own",
    )(live, q, g, k, e, dp, near, given, dqc, dkc, dvc)


def spread(terms, count):
    return pl.pallas_call(
        spread_kernel,
        out_shape=pltpu.HBM((count,) + terms.shape[1:], jnp.float32),
        out_specs=VMEM,
        compiler_params=params(),
        cost_estimate=COST,
        name="spread",
    )(terms)


def sum_over_devices(parts, inner, outer, heads, after):
    count = parts.shape[0]
    terms = lax.all_to_all(parts, inner, 0, 0)
    sums = spread(terms, count * lax.axis_size(outer))
    every = lax.all_to_all(sums, (inner, outer), 0, 0)
    return pl.pallas_call(
        functools.partial(gather_kernel, count),
        in_specs=[VMEM, ANY],
        out_shape=shape((heads, 3 * BLOCK)),
        compiler_params=params(),
        cost_estimate=COST,
        name="gather",
    )(every, pltpu.with_memory_space_constraint(after, pltpu.HBM))


def per_device(queries, keys, values, out_grad, lengths, rel_bias):
    frame_count, feature_width = queries.shape[1:]
    head_count = rel_bias.shape[0]
    head_width = feature_width // head_count
    groups = head_count // GROUP_HEADS
    live_own = lengths - lax.axis_index("tm") * BLOCK
    live_next = live_own - BLOCK
    q, k, v, g = (a.reshape(frame_count, feature_width) for a in (queries, keys, values, out_grad))

    q_next = shifted(q, "tm", -1)
    *before, chunk, w = own_stats(head_width, 0, live_own, q, g, k, v, rel_bias, ())
    chunks = [shifted(chunk, "tm", -1)]
    for group in range(1, groups):
        *before, chunk = own_stats(head_width, group, live_own, q, g, k, v, w, before)
        chunks.append(shifted(chunk, "tm", -1))
    near, e, dp = before
    results = ()
    for group in range(groups):
        results = cross(head_width, group, live_next, q_next, chunks[group], k, v, w, results)
    given, dq_cross, dkc, dvc, lines = results
    given = shifted(given, "tm", 1)
    dq_cross = shifted(dq_cross, "tm", 1)
    parts = lax.axis_size("dp")
    table = table_sums(e, dp, near, given, lines, parts)
    late = (pltpu.with_memory_space_constraint(a, pltpu.HBM) for a in (e, dp, near, given))
    dq, dk, dv = own(head_width, live_own, q, g, k, *late, dq_cross, dkc, dvc)
    bias_grad = sum_over_devices(table, "dp", "tm", head_count, dq)
    return tuple(a[None] for a in (dq, dk, dv)) + (bias_grad,)


def solution(mesh):
    block = P("dp", "tm", None)
    return jax.shard_map(
        per_device,
        mesh=mesh,
        in_specs=(block, block, block, block, P("dp"), P()),
        out_specs=(block, block, block, P()),
        check_vma=False,
    )
```
